32 devices in a mesh: branch: 4 (over y, x), row: 8 (over z, core).
Axes of the slice: x: 2, y: 2, z: 4, core: 2. Of those that a mesh axis runs over, the one named last changes fastest.
Arguments:
- root_cov: bfloat16 [2304, 2304], P('row', 'branch')
- diag_factor: float32 [4, 3, 576, 576], P('branch')
- panel_factor: float32 [4, 3, 2304, 576], P('branch', None, 'row'), may hold values from -0.009765625 to 0.009765625
- chain_factor: float32 [4, 2, 576, 576], P('branch'), may hold values from -0.25 to 0.25
- panel_tiles: int32 [4, 3], P('branch'), may hold values from 0 to 3, as said below
Outputs:
- panel_cov: float32 [4, 3, 2304, 576], P('branch', None, 'row')
- block_cov: float32 [4, 5, 576, 576], P('branch')
The draws below stay inside these ranges and needn't reach their ends.
Inputs may be any that keep to these rules, and one draw needn't show every extreme that they name: `panel_tiles`: the entries of a row are distinct; the first 2 and the first 1 entries of a row are the level-two and level-three patterns.
All inputs are finite; a program needn't handle non-finite values.
Results may differ from the reference program's by a relative error of at most 0.0029.
Values may be sent and summed in bfloat16 or wider, within the bound.
A program may use at most 192 MiB of HBM per device.

```python
import math
import jax
import jax.numpy as jnp
from jax import lax

W = 576
RT = 4
NR = 2304
K1 = 3
K2 = 2
K3 = 1
N_BRANCH = 4


def draw_root_cov(key, part):
    noise = jax.random.normal(key, (NR, NR), jnp.float32)
    spread = jax.random.uniform(jax.random.fold_in(key, 7), (NR,), jnp.float32, 1.0, 2.0)
    offdiag = (noise + noise.T) * (0.5 / math.sqrt(2.0 * NR))
    return (W * (offdiag + jnp.diag(spread))).astype(jnp.bfloat16)


def draw_diag_factor(key, part):
    noise = jax.random.normal(key, (N_BRANCH, 3, W, W), jnp.float32)
    spread = jax.random.uniform(jax.random.fold_in(key, 11), (N_BRANCH, 3, W, 1), jnp.float32, 1.0, 2.0)
    lower = jnp.tril(noise, -1) * (0.5 / math.sqrt(1.0 * W))
    identity = jnp.eye(W, dtype=jnp.float32)
    return lower + identity * spread


def draw_panel_tiles(key, part):
    keys = jax.random.split(key, N_BRANCH)
    orders = jax.vmap(lambda single: jax.random.permutation(single, RT))(keys)
    return orders[:, :K1].astype(jnp.int32)


def level_of(own_key, extent, pieces, least, largest):
    factor_of, own = 1.0, jax.random.fold_in(own_key, 6)
    for dim, shards_of in pieces:
        steps = jnp.exp(jax.random.uniform(jax.random.fold_in(own, dim), (shards_of,), jnp.float32, least / len(pieces), largest / len(pieces)))
        factor_of = factor_of * jnp.repeat(steps, extent[dim] // shards_of).reshape([-1 if axis == dim else 1 for axis in range(len(extent))])
    return factor_of


def normal_values(rng, dims, deviation, reach, shards=(), kind=jnp.bfloat16):
    level = level_of(rng, dims, shards, -0.22, 0.18) if shards else 1.0
    values = jax.random.normal(rng, dims, jnp.float32) * deviation * level
    return jnp.minimum(jnp.maximum(values, -reach), reach).astype(kind)


def setup_inputs(seed: int = 0) -> dict:
    splits = jax.random.split(jax.random.key(seed), 6)
    return {
        "root_cov": draw_root_cov(jax.random.fold_in(splits[5], 71), 0),
        "diag_factor": draw_diag_factor(jax.random.fold_in(splits[5], 71), 0),
        "panel_factor": normal_values(splits[2], (N_BRANCH, 3, NR, W), (W * W) ** -0.5, 0.009765625, ((0, 4), (2, 8)), jnp.float32),
        "chain_factor": normal_values(splits[3], (N_BRANCH, 2, W, W), W ** -0.5, 0.25, ((0, 4),), jnp.float32),
        "panel_tiles": draw_panel_tiles(jax.random.fold_in(splits[5], 71), 0),
    }


HIGHEST = lax.Precision.HIGHEST

def product(left_mat, right_mat):
    return jnp.dot(left_mat.astype(jnp.float32), right_mat.astype(jnp.float32), precision=HIGHEST, preferred_element_type=jnp.float32)

def reference(root_cov, diag_factor, panel_factor, chain_factor, panel_tiles):
    identity = jnp.eye(W, dtype=jnp.float32)
    tile_of_row = (jnp.arange(NR) // W).astype(jnp.int32)
    root_wide = root_cov.astype(jnp.float32)
    counts = (K1, K2, K3)
    panels = [[] for branch_index in range(N_BRANCH)]
    blocks = [[] for branch_index in range(N_BRANCH)]
    crosses = [[] for branch_index in range(N_BRANCH)]
    for layer_index in range(3):
        inverses = []
        chosen_all = []
        scaled_all = []
        for branch_index in range(N_BRANCH):
            inverse = jax.scipy.linalg.solve_triangular(diag_factor[branch_index, layer_index], identity, lower=True)
            chosen = jnp.any(tile_of_row[:, None] == panel_tiles[branch_index, :counts[layer_index]][None, :], axis=1)
            scaled = jnp.where(chosen[:, None], product(panel_factor[branch_index, layer_index], inverse), 0.0)
            inverses.append(inverse)
            chosen_all.append(chosen)
            scaled_all.append(scaled)
        rounded = jnp.concatenate([lax.optimization_barrier(item.astype(jnp.bfloat16)).astype(jnp.float32) for item in scaled_all], axis=1)
        projected = product(root_wide, rounded)
        for branch_index in range(N_BRANCH):
            inverse = inverses[branch_index]
            gram = product(inverse.T, inverse)
            chosen = chosen_all[branch_index]
            scaled = scaled_all[branch_index]
            gathered = projected[:, branch_index * W:(branch_index + 1) * W]
            if layer_index == 0:
                panel = -jnp.where(chosen[:, None], gathered, 0.0)
                block = gram - product(scaled.T, panel)
            else:
                previous_panel = panels[branch_index][-1]
                previous_block = blocks[branch_index][-1]
                scaled_chain = product(chain_factor[branch_index, layer_index - 1], inverse)
                panel = -jnp.where(chosen[:, None], gathered + product(previous_panel, scaled_chain), 0.0)
                cross = -(product(previous_panel.T, scaled) + product(previous_block, scaled_chain))
                block = gram - product(scaled.T, panel) - product(scaled_chain.T, cross)
                crosses[branch_index].append(cross)
            panels[branch_index].append(panel)
            blocks[branch_index].append(block)
    panel_cov = jnp.stack([jnp.stack(panels[branch_index]) for branch_index in range(N_BRANCH)])
    block_cov = jnp.stack([jnp.stack(blocks[branch_index] + crosses[branch_index]) for branch_index in range(N_BRANCH)])
    return (panel_cov, block_cov)
```

```python
import functools
import jax
import jax.numpy as jnp
from jax import lax
from jax.experimental import pallas as pl
from jax.experimental.pallas import tpu as pltpu
from jax.sharding import PartitionSpec as P

BF = jnp.bfloat16
F32 = jnp.float32
MESH = pl.DeviceIdType.MESH


def product(left_mat, right_mat):
    return jnp.dot(left_mat, right_mat, precision=lax.Precision.HIGH, preferred_element_type=F32)


def split(x):
    hi = x.astype(BF)
    return hi, (x - hi.astype(F32)).astype(BF)


def mm(a, b):
    return jnp.dot(a, b, preferred_element_type=F32)


def dot3(a, b):
    a_hi, a_lo = a
    b_hi, b_lo = b
    return mm(a_hi, b_hi) + (mm(a_lo, b_hi) + mm(a_hi, b_lo))


def inverse_kernel(size, window, l_ref, out_ref):
    count = size // window
    row = lax.broadcasted_iota(jnp.int32, (window, window), 0)
    col = lax.broadcasted_iota(jnp.int32, (window, window), 1)
    eye = row == col
    diagonals = []
    for w in range(count):
        at = slice(w * window, (w + 1) * window)
        block = l_ref[0, 0, at, at]
        kept = jnp.where(eye, block, 0.0)
        down = 1.0 / jnp.sum(kept, axis=1, keepdims=True)
        across = 1.0 / jnp.sum(kept, axis=0, keepdims=True)
        diagonals.append((block * down, across))
    found = []
    for scaled, across in diagonals:
        x = jnp.where(eye, 1.0, 0.0)
        x = x - jnp.where((row // 2 == col // 2) & (row > col), scaled, 0.0)
        found.append(x)
    k = 2
    while k < window:
        pair = (row // (2 * k) == col // (2 * k)) & (row // k > col // k)
        for w in range(count):
            x = found[w]
            parts = split(x)
            right = dot3(split(jnp.where(pair, diagonals[w][0], 0.0)), parts)
            found[w] = x - dot3(parts, split(right))
        k *= 2
    found = [x * diagonals[w][1] for w, x in enumerate(found)]
    done = {}
    for w in range(count):
        done[w, w] = split(found[w])
        out_ref[0, w * window:(w + 1) * window, w * window:(w + 1) * window] = found[w]
    for gap in range(1, count):
        for c in range(count - gap):
            r = c + gap
            total = None
            for m in range(c, r):
                below = split(l_ref[0, 0, r * window:(r + 1) * window, m * window:(m + 1) * window])
                term = dot3(below, done[m, c])
                total = term if total is None else total + term
            value = -dot3(done[r, r], split(total))
            done[r, c] = split(value)
            out_ref[0, r * window:(r + 1) * window, c * window:(c + 1) * window] = value
            out_ref[0, c * window:(c + 1) * window, r * window:(r + 1) * window] = jnp.zeros(
                (window, window), F32
            )


def inverses(diag_factor):
    levels, size = diag_factor.shape[1], diag_factor.shape[-1]
    return pl.pallas_call(
        functools.partial(inverse_kernel, size, size // 3),
        grid=(levels,),
        in_specs=[pl.BlockSpec((1, 1, size, size), lambda i: (0, i, 0, 0))],
        out_specs=pl.BlockSpec((1, size, size), lambda i: (i, 0, 0)),
        out_shape=jax.ShapeDtypeStruct((levels, size, size), F32),
        compiler_params=pltpu.CompilerParams(vmem_limit_bytes=48 * 2**20),
        name="inverses",
    )(diag_factor)


def sum_kernel(x_ref, out_ref, pair, send, landed, right_got, left_got, right_sib, left_sib, final,
               final_sib, pair_s, pair_r, rs_s, rs_r, right_s, right_r, left_s, left_r, sib_s, sib_r):
    me = lax.axis_index("row")
    z = me // 2
    core = me % 2
    sibling = 2 * z + 1 - core

    def at_chip(chip):
        return {"row": 2 * chip + core}

    barrier = pltpu.get_barrier_semaphore()
    pl.semaphore_signal(barrier, inc=1, device_id={"row": sibling}, device_id_type=MESH)
    for k in (1, 2, 3):
        pl.semaphore_signal(
            barrier, inc=1, device_id=at_chip((z + k) % 4), device_id_type=MESH
        )
    pl.semaphore_wait(barrier, 4)

    def copy(src, dst, send_sem, recv_sem, target):
        return pltpu.make_async_remote_copy(
            src_ref=src, dst_ref=dst, send_sem=send_sem, recv_sem=recv_sem,
            device_id=target, device_id_type=MESH,
        )

    to_pair = {}
    for k in (2, 1, 3, 0):
        to_pair[k] = copy(
            x_ref.at[1 - core, (z + k) % 4], pair.at[k], pair_s.at[k], pair_r.at[k],
            {"row": sibling},
        )
        to_pair[k].start()
    scatter = {}
    for k in (2, 1, 3):
        to_pair[k].wait_recv()
        send[k - 1] = (x_ref[core, (z + k) % 4] + pair[k]).astype(BF)
        scatter[k] = copy(
            send.at[k - 1], landed.at[k - 1], rs_s.at[k - 1], rs_r.at[k - 1],
            at_chip((z + k) % 4),
        )
        scatter[k].start()
    to_pair[0].wait_recv()
    pair[0] = pair[0] + x_ref[core, z]
    for k in (1, 3, 2):
        scatter[k].wait_recv()
        pair[0] = pair[0] + landed[k - 1].astype(F32)
    final[...] = pair[0].astype(BF)

    rights, lefts, sibs = {}, {}, {}
    sibs[0] = copy(final, final_sib, sib_s.at[0], sib_r.at[0], {"row": sibling})
    for s in (1, 2, 3):
        rights[s] = copy(
            final if s == 1 else right_got.at[s - 2], right_got.at[s - 1],
            right_s.at[s - 1], right_r.at[s - 1], at_chip(jnp.minimum(z + 1, 3)),
        )
        lefts[s] = copy(
            final if s == 1 else left_got.at[s - 2], left_got.at[s - 1],
            left_s.at[s - 1], left_r.at[s - 1], at_chip(jnp.maximum(z - 1, 0)),
        )
        sibs[s] = copy(
            right_got.at[s - 1], right_sib.at[s - 1], sib_s.at[s], sib_r.at[s], {"row": sibling}
        )
        sibs[-s] = copy(
            left_got.at[s - 1], left_sib.at[s - 1], sib_s.at[3 + s], sib_r.at[3 + s],
            {"row": sibling},
        )

    def goes_right(s):
        return (z < 3) & (z >= s - 1)

    def goes_left(s):
        return (z > 0) & (z + s <= 4)

    pl.when(goes_right(1))(rights[1].start)
    pl.when(goes_left(1))(lefts[1].start)
    sibs[0].start()
    out_ref[core, z] = pair[0]
    for s in (1, 2, 3):
        @pl.when(z >= s)
        def _():
            rights[s].wait_recv()
            sibs[s].start()

        if s < 3:
            pl.when(goes_right(s + 1))(rights[s + 1].start)

        @pl.when(z + s <= 3)
        def _():
            lefts[s].wait_recv()
            sibs[-s].start()

        if s < 3:
            pl.when(goes_left(s + 1))(lefts[s + 1].start)

        @pl.when(z >= s)
        def _():
            out_ref[core, z - s] = right_got[s - 1].astype(F32)

        @pl.when(z + s <= 3)
        def _():
            out_ref[core, z + s] = left_got[s - 1].astype(F32)

    sibs[0].wait_recv()
    out_ref[1 - core, z] = final_sib[...].astype(F32)
    for s in (1, 2, 3):
        @pl.when(z >= s)
        def _():
            sibs[s].wait_recv()
            out_ref[1 - core, z - s] = right_sib[s - 1].astype(F32)

        @pl.when(z + s <= 3)
        def _():
            sibs[-s].wait_recv()
            out_ref[1 - core, z + s] = left_sib[s - 1].astype(F32)

    for k in (0, 1, 2, 3):
        to_pair[k].wait_send()
        if k:
            scatter[k].wait_send()
    sibs[0].wait_send()
    for s in (1, 2, 3):
        pl.when(goes_right(s))(rights[s].wait_send)
        pl.when(goes_left(s))(lefts[s].wait_send)
        pl.when(z >= s)(sibs[s].wait_send)
        pl.when(z + s <= 3)(sibs[-s].wait_send)


def line_sum(x, total):
    rows, columns = x.shape[0] // 8, x.shape[1]
    dma = pltpu.SemaphoreType.DMA
    whole = pl.BlockSpec(memory_space=pltpu.VMEM)
    out = pl.pallas_call(
        sum_kernel,
        out_shape=jax.ShapeDtypeStruct((2, 4, rows, columns), F32),
        in_specs=[whole],
        out_specs=whole,
        scratch_shapes=[
            pltpu.VMEM((4, rows, columns), F32),
            *[pltpu.VMEM((3, rows, columns), BF) for _ in range(6)],
            pltpu.VMEM((rows, columns), BF),
            pltpu.VMEM((rows, columns), BF),
            dma((4,)), dma((4,)),
            *[dma((3,)) for _ in range(6)],
            dma((7,)), dma((7,)),
        ],
        compiler_params=pltpu.CompilerParams(
            collective_id=0, has_side_effects=True, vmem_limit_bytes=48 * 2**20
        ),
        name="line_sum",
    )(x.reshape(2, 4, rows, columns))
    return out.reshape(8 * rows, columns)[:total]


def gather_kernel(x_ref, out_ref, right_s, right_r, left_s, left_r, sib_s, sib_r, own_s):
    me = lax.axis_index("row")
    z = me // 2
    core = me % 2
    sibling = 2 * z + 1 - core
    right = 2 * jnp.minimum(z + 1, 3) + core
    left = 2 * jnp.maximum(z - 1, 0) + core
    barrier = pltpu.get_barrier_semaphore()
    pl.semaphore_signal(barrier, inc=1, device_id={"row": sibling}, device_id_type=MESH)
    for k in (1, 2, 3):
        pl.semaphore_signal(
            barrier, inc=1, device_id={"row": 2 * ((z + k) % 4) + core}, device_id_type=MESH
        )
    pl.semaphore_wait(barrier, 4)

    def moved(source, part, send_sem, recv_sem, target, first):
        return pltpu.make_async_remote_copy(
            src_ref=x_ref.at[part] if first else out_ref.at[source, part],
            dst_ref=out_ref.at[source, part], send_sem=send_sem, recv_sem=recv_sem,
            device_id={"row": target}, device_id_type=MESH,
        )

    steps = [(s, p) for s in (1, 2, 3) for p in (0, 1)]
    rights, lefts, sib_right, sib_left, own = {}, {}, {}, {}, {}
    for p in (0, 1):
        own[p] = moved(me, p, sib_s.at[0, p], sib_r.at[0, p], sibling, True)
    for s, p in steps:
        from_left = 2 * jnp.maximum(z - s, 0) + core
        from_right = 2 * jnp.minimum(z + s, 3) + core
        rights[s, p] = moved(
            2 * jnp.maximum(z - s + 1, 0) + core, p, right_s.at[s - 1, p], right_r.at[s - 1, p],
            right, s == 1,
        )
        lefts[s, p] = moved(
            2 * jnp.minimum(z + s - 1, 3) + core, p, left_s.at[s - 1, p], left_r.at[s - 1, p],
            left, s == 1,
        )
        sib_right[s, p] = moved(from_left, p, sib_s.at[s, p], sib_r.at[s, p], sibling, False)
        sib_left[s, p] = moved(
            from_right, p, sib_s.at[3 + s, p], sib_r.at[3 + s, p], sibling, False
        )

    def goes_right(s):
        return (z < 3) & (z >= s - 1)

    def goes_left(s):
        return (z > 0) & (z + s <= 4)

    for p in (0, 1):
        pl.when(goes_right(1))(rights[1, p].start)
        pl.when(goes_left(1))(lefts[1, p].start)
    for p in (0, 1):
        own[p].start()
    keep = pltpu.make_async_copy(x_ref, out_ref.at[me], own_s)
    keep.start()
    for s, p in steps:
        @pl.when(z >= s)
        def _():
            rights[s, p].wait_recv()
            sib_right[s, p].start()

        if s < 3:
            pl.when(goes_right(s + 1))(rights[s + 1, p].start)

        @pl.when(z + s <= 3)
        def _():
            lefts[s, p].wait_recv()
            sib_left[s, p].start()

        if s < 3:
            pl.when(goes_left(s + 1))(lefts[s + 1, p].start)
    keep.wait()
    for p in (0, 1):
        own[p].wait()
    for s, p in steps:
        pl.when(goes_right(s))(rights[s, p].wait_send)
        pl.when(goes_left(s))(lefts[s, p].wait_send)
        pl.when(z >= s)(sib_right[s, p].wait)
        pl.when(z + s <= 3)(sib_left[s, p].wait)


def line_gather(x):
    dma = pltpu.SemaphoreType.DMA
    whole = pl.BlockSpec(memory_space=pltpu.VMEM)
    return pl.pallas_call(
        gather_kernel,
        out_shape=jax.ShapeDtypeStruct((8, *x.shape), x.dtype),
        in_specs=[whole],
        out_specs=whole,
        scratch_shapes=[*[dma((3, 2)) for _ in range(4)], dma((7, 2)), dma((7, 2)), dma(())],
        compiler_params=pltpu.CompilerParams(
            collective_id=1, has_side_effects=True, vmem_limit_bytes=32 * 2**20
        ),
        name="line_gather",
    )(x)


def dot3t(a, b):
    def one(p, q):
        return lax.dot_general(p, q, (((0,), (0,)), ((), ())), preferred_element_type=F32)

    return one(a[0], b[0]) + (one(a[1], b[0]) + one(a[0], b[1]))


def partial_kernel(size, keep_ref, root_ref, all_ref, pair_ref, scaled_ref, mine_ref, chain_ref,
                   panel_ref, part_ref):
    tile = lax.axis_index("row") // 2
    panel = block = None
    for i in range(3):
        if i < 2:
            projected = None
            for b in range(4):
                term = mm(root_ref[b], all_ref[2 * b:2 * b + 2, i].reshape(size, size))
                projected = term if projected is None else projected + term
        else:
            projected = mm(root_ref[tile], pair_ref[...])
        scaled = split(scaled_ref[i])
        mine = split(mine_ref[i])
        if i:
            chain = split(chain_ref[i - 1])
            projected = projected + dot3(panel, chain)
            cross = -(dot3t(panel, scaled) + dot3(block, chain))
            part_ref[(2 + i) * size:(3 + i) * size] = cross
        kept = jnp.where(keep_ref[i] > 0, -projected, 0.0)
        panel_ref[0, i] = kept
        panel = split(kept)
        value = dot3t(mine, mine) - dot3t(scaled, panel)
        if i:
            value = value - dot3t(chain, split(cross))
        part_ref[i * size:(i + 1) * size] = value
        block = split(value)
    rest = part_ref.shape[0] - 5 * size
    part_ref[5 * size:] = jnp.zeros((rest, size), F32)


def partials(keep, root, everyone, pair, scaled, mine, chain):
    size = scaled.shape[-1]
    rows = -(-5 * size // 128) * 128
    whole = pl.BlockSpec(memory_space=pltpu.VMEM)
    return pl.pallas_call(
        functools.partial(partial_kernel, size),
        out_shape=(
            jax.ShapeDtypeStruct((1, *scaled.shape), F32),
            jax.ShapeDtypeStruct((rows, size), F32),
        ),
        in_specs=[pl.BlockSpec(memory_space=pltpu.SMEM)] + [whole] * 6,
        out_specs=(whole, whole),
        compiler_params=pltpu.CompilerParams(vmem_limit_bytes=52 * 2**20),
        name="partials",
    )(keep, root, everyone, pair, scaled, mine, chain)


def on_device(root_cov, diag_factor, panel_factor, chain_factor, panel_tiles):
    node_width = diag_factor.shape[-1]
    rows_here = panel_factor.shape[2]
    per_tile = node_width // rows_here
    row_count = lax.axis_size("row")
    tile_total = row_count // per_tile
    counts = (3 * tile_total // 4, tile_total // 2, tile_total // 4)
    small = row_count == 8 and tile_total == 4 and root_cov.shape[1] == node_width
    if small:
        root_rows = lax.all_gather(root_cov, "branch")
    else:
        root_rows = lax.all_gather(root_cov, "branch", axis=1, tiled=True)
    me = lax.axis_index("row")
    my_tile = me // per_tile
    inverse_all = inverses(diag_factor)
    share = -(-node_width // row_count // 8) * 8
    padded = jnp.pad(inverse_all, ((0, 0), (0, share * row_count - node_width), (0, 0)))
    mine = lax.dynamic_slice_in_dim(padded, me * share, share, axis=1)
    chosen = [jnp.any(panel_tiles[0, : counts[i]] == my_tile) for i in range(3)]
    scaled = [
        jnp.where(chosen[i], product(panel_factor[0, i], inverse_all[i]), 0.0) for i in range(3)
    ]
    if small:
        rounded = [x.astype(BF) for x in scaled]
        theirs = lax.ppermute(rounded[2], "row", [(d, d ^ 1) for d in range(row_count)])
        pair = jnp.where(
            me % 2 == 0,
            jnp.concatenate([rounded[2], theirs]),
            jnp.concatenate([theirs, rounded[2]]),
        )
        everyone = line_gather(jnp.stack(rounded[:2]))
        chain_all = jnp.stack([product(chain_factor[0, i - 1], inverse_all[i]) for i in (1, 2)])
        panel_out, parts = partials(
            jnp.stack(chosen).astype(jnp.int32), root_rows, everyone, pair, jnp.stack(scaled),
            mine, chain_all,
        )
        total = line_sum(parts, 5 * node_width)
        return (panel_out, total.reshape(1, 5, node_width, node_width))
    panels = []
    blocks = []
    crosses = []
    for i in range(3):
        rounded = scaled[i].astype(BF)
        gathered = jnp.dot(
            root_rows,
            lax.all_gather(rounded, "row", axis=0, tiled=True),
            preferred_element_type=F32,
        )
        left = jnp.concatenate([mine[i], scaled[i]], axis=0)
        if i == 0:
            panel = -jnp.where(chosen[i], gathered, 0.0)
            block = product(left.T, jnp.concatenate([mine[i], -panel], axis=0))
        else:
            chain = product(chain_factor[0, i - 1], inverse_all[i])
            panel = -jnp.where(chosen[i], gathered + product(panels[-1], chain), 0.0)
            cross = -(product(panels[-1].T, scaled[i]) + product(blocks[-1], chain))
            block = product(left.T, jnp.concatenate([mine[i], -panel], axis=0)) - product(
                chain.T, cross
            )
            crosses.append(cross)
        panels.append(panel)
        blocks.append(block)
    total = lax.psum(jnp.stack(blocks + crosses), "row")
    return (jnp.stack(panels)[None], total[None])


def solution(mesh):
    in_specs = (
        P("row", "branch"),
        P("branch", None, None, None),
        P("branch", None, "row", None),
        P("branch", None, None, None),
        P("branch", None),
    )
    out_specs = (P("branch", None, "row", None), P("branch", None, None, None))
    return jax.shard_map(
        on_device, mesh=mesh, in_specs=in_specs, out_specs=out_specs, check_vma=False
    )
```

```python
import functools
import jax
import jax.numpy as jnp
from jax import lax
from jax.experimental import pallas as pl
from jax.experimental.pallas import tpu as pltpu
from jax.sharding import PartitionSpec as P

BF = jnp.bfloat16
F32 = jnp.float32
MESH = pl.DeviceIdType.MESH


def product(left_mat, right_mat):
    return jnp.dot(left_mat, right_mat, precision=lax.Precision.HIGH, preferred_element_type=F32)


def split(x):
    hi = x.astype(BF)
    return hi, (x - hi.astype(F32)).astype(BF)


def mm(a, b):
    return jnp.dot(a, b, preferred_element_type=F32)


def dot3(a, b):
    a_hi, a_lo = a
    b_hi, b_lo = b
    return mm(a_hi, b_hi) + (mm(a_lo, b_hi) + mm(a_hi, b_lo))


def inverse_kernel(size, window, l_ref, out_ref):
    count = size // window
    row = lax.broadcasted_iota(jnp.int32, (window, window), 0)
    col = lax.broadcasted_iota(jnp.int32, (window, window), 1)
    eye = row == col
    diagonals = []
    for w in range(count):
        at = slice(w * window, (w + 1) * window)
        block = l_ref[0, 0, at, at]
        kept = jnp.where(eye, block, 0.0)
        down = 1.0 / jnp.sum(kept, axis=1, keepdims=True)
        across = 1.0 / jnp.sum(kept, axis=0, keepdims=True)
        diagonals.append((block * down, across))
    found = []
    for scaled, across in diagonals:
        x = jnp.where(eye, 1.0, 0.0)
        x = x - jnp.where((row // 2 == col // 2) & (row > col), scaled, 0.0)
        found.append(x)
    k = 2
    while k < window:
        pair = (row // (2 * k) == col // (2 * k)) & (row // k > col // k)
        for w in range(count):
            x = found[w]
            parts = split(x)
            right = dot3(split(jnp.where(pair, diagonals[w][0], 0.0)), parts)
            found[w] = x - dot3(parts, split(right))
        k *= 2
    found = [x * diagonals[w][1] for w, x in enumerate(found)]
    done = {}
    for w in range(count):
        done[w, w] = split(found[w])
        out_ref[0, w * window:(w + 1) * window, w * window:(w + 1) * window] = found[w]
    for gap in range(1, count):
        for c in range(count - gap):
            r = c + gap
            total = None
            for m in range(c, r):
                below = split(l_ref[0, 0, r * window:(r + 1) * window, m * window:(m + 1) * window])
                term = dot3(below, done[m, c])
                total = term if total is None else total + term
            value = -dot3(done[r, r], split(total))
            done[r, c] = split(value)
            out_ref[0, r * window:(r + 1) * window, c * window:(c + 1) * window] = value
            out_ref[0, c * window:(c + 1) * window, r * window:(r + 1) * window] = jnp.zeros(
                (window, window), F32
            )


def inverses(diag_factor):
    levels, size = diag_factor.shape[1], diag_factor.shape[-1]
    return pl.pallas_call(
        functools.partial(inverse_kernel, size, size // 3),
        grid=(levels,),
        in_specs=[pl.BlockSpec((1, 1, size, size), lambda i: (0, i, 0, 0))],
        out_specs=pl.BlockSpec((1, size, size), lambda i: (i, 0, 0)),
        out_shape=jax.ShapeDtypeStruct((levels, size, size), F32),
        compiler_params=pltpu.CompilerParams(vmem_limit_bytes=48 * 2**20),
        name="inverses",
    )(diag_factor)


def nt(a, b):
    return lax.dot_general(a, b, (((1,), (1,)), ((), ())), preferred_element_type=F32)


def nt3(a, b):
    return nt(a[0], b[0]) + (nt(a[1], b[0]) + nt(a[0], b[1]))


def inverse_steps(low, inv, level, starts):
    found, scaled, downs, pairs, eyes = [], [], [], [], []
    for at, to in starts:
        span = to - at
        row = lax.broadcasted_iota(jnp.int32, (span, span), 0)
        col = lax.broadcasted_iota(jnp.int32, (span, span), 1)
        eye = row == col
        block = low[level, at:to, at:to]
        down = 1.0 / jnp.sum(jnp.where(eye, block, 0.0), axis=1, keepdims=True)
        scaled.append(jnp.where(row > col, block * down, 0.0))
        downs.append(down)
        pairs.append(row ^ col)
        eyes.append(jnp.where(eye, 1.0, 0.0))
        first = split(jnp.where(pairs[-1] == 1, scaled[-1], 0.0))
        unit = eyes[-1].astype(BF)
        found.append(eyes[-1] - (nt(unit, first[0]) + nt(unit, first[1])))
    yield
    k = 2
    while k < starts[0][1] - starts[0][0]:
        for w, (at, to) in enumerate(starts):
            if k < to - at:
                parts = split(found[w])
                pair = (pairs[w] >= k) & (pairs[w] < 2 * k)
                right = nt3(parts, split(jnp.where(pair, scaled[w], 0.0)))
                found[w] = found[w] - dot3(split(right), parts)
        k *= 2
        yield
    done = {}

    def keep(c, r, value):
        done[c, r] = split(value)
        rows, columns = slice(*starts[c]), slice(*starts[r])
        inv[0, level, rows, columns] = done[c, r][0]
        inv[1, level, rows, columns] = done[c, r][1]

    for w in range(len(starts)):
        keep(w, w, found[w] * downs[w])
    for gap in range(1, len(starts)):
        for c in range(len(starts) - gap):
            r = c + gap
            total = None
            for m in range(c, r):
                below = split(low[level, slice(*starts[r]), slice(*starts[m])])
                term = nt3(done[c, m], below)
                total = term if total is None else total + term
            keep(c, r, -dot3(split(total), done[r, r]))
            zero = jnp.zeros((starts[r][1] - starts[r][0], starts[c][1] - starts[c][0]), BF)
            inv[0, level, slice(*starts[r]), slice(*starts[c])] = zero
            inv[1, level, slice(*starts[r]), slice(*starts[c])] = zero
        yield


def whole_kernel(size, tiles, root_in, low_in, panel_in, chain_in, panel_out, block_out,
                 low, pf, ch, root, inv, sc, ct, pt, acc, gram, g1, g1s, g2, g2s, ar, ars,
                 load_s, pf_s, pf_r, root_s, root_r, fwd_s, fwd_r, sc_s, sc_r, pt_s, pt_r,
                 a_s, a_r, b_s, b_r, x_s, v_s, v_r, out_s, out_r):
    half = size // 2
    parts = 3
    step = half // parts
    branch = lax.axis_index("branch")
    me = lax.axis_index("row")
    z = me // 2
    core = me % 2
    side = z // 2
    outer, near, across, beyond = 3 * side, 1 + side, 2 - side, 3 - 3 * side
    is_inner = z == near
    is_outer = z == outer
    own = pl.ds(pl.multiple_of(core * half, 32), half)
    sibling = {"row": 2 * z + 1 - core}

    def chip(at):
        return {"row": 2 * at + core}

    def copy(src, dst, send_sem, recv_sem, target):
        return pltpu.make_async_remote_copy(
            src_ref=src, dst_ref=dst, send_sem=send_sem, recv_sem=recv_sem,
            device_id=target, device_id_type=MESH,
        )

    barrier = pltpu.get_barrier_semaphore()
    peers = [sibling] + [chip((z + k) % 4) for k in (1, 2, 3)]
    peers += [{"branch": (branch + k) % 4} for k in (1, 2, 3)]
    for peer in peers:
        pl.semaphore_signal(barrier, inc=1, device_id=peer, device_id_type=MESH)

    loads = {}
    for i in range(3):
        loads["low", i] = pltpu.make_async_copy(low_in.at[0, i], low.at[i], load_s.at[i])
        loads["pf", i] = pltpu.make_async_copy(
            panel_in.at[0, i], pf.at[i, own], load_s.at[3 + i]
        )
    loads["ch", 0] = pltpu.make_async_copy(chain_in.at[0], ch, load_s.at[6])
    loads["root", 0] = pltpu.make_async_copy(root_in, root.at[branch, own], load_s.at[7])
    for key in (("low", 0), ("pf", 0), ("root", 0), ("low", 1), ("low", 2), ("pf", 1), ("pf", 2),
                ("ch", 0)):
        loads[key].start()
    pl.semaphore_wait(barrier, 7)

    pf_to = [
        copy(panel_in.at[0, i], pf.at[i, own], pf_s.at[i], pf_r.at[i], sibling) for i in range(3)
    ]
    root_to = [
        copy(root_in, root.at[branch, own], root_s.at[k - 1], root_r.at[k - 1],
             {"branch": (branch + k) % 4})
        for k in (1, 2, 3)
    ]
    root_own = copy(root_in, root.at[branch, own], fwd_s.at[0], fwd_r.at[0], sibling)
    root_on = []
    for k in (1, 2, 3):
        block = root.at[(branch + 4 - k) % 4, own]
        root_on.append(copy(block, block, fwd_s.at[k], fwd_r.at[k], sibling))
    pf_to[0].start()
    for k in range(3):
        root_to[k].start()
    root_own.start()
    pf_to[1].start()
    pf_to[2].start()

    first, second, third = tiles[0, 0], tiles[0, 1], tiles[0, 2]

    def among(tile, count):
        hit = tile == first
        if count > 1:
            hit = hit | (tile == second)
        if count > 2:
            hit = hit | (tile == third)
        return jnp.where(hit, 1.0, 0.0)

    kept = [among(z, 3), among(z, 2), among(z, 1)]
    near_in, beyond_in = among(near, 3), among(beyond, 3)
    a_index = jnp.where(is_outer & (beyond_in < 0.5), across, beyond)
    b_index = jnp.where(is_outer & (near_in > 0.5), near, across)
    other_index = jnp.where(z == first, second, first)

    bounds = list(range(0, size, 256)) + [size]
    starts = list(zip(bounds[:-1], bounds[1:]))

    def rows(k):
        return slice(k * step, (k + 1) * step)

    def own_rows(k):
        return pl.ds(pl.multiple_of(core * half + k * step, 32), step)

    def both(ref, *index):
        return ref[(0, *index)], ref[(1, *index)]

    def keep(ref, index, value):
        hi, lo = split(value)
        ref[(0, *index)] = hi
        ref[(1, *index)] = lo

    a_far = [copy(sc.at[0, 0, own_rows(k)], g1.at[1, rows(k)], a_s.at[0, k], a_r.at[1, k],
                  chip(across)) for k in range(parts)]
    a_near = [copy(sc.at[0, 0, own_rows(k)], g1.at[0, rows(k)], a_s.at[1, k], a_r.at[0, k],
                   chip(near)) for k in range(parts)]
    b_far = [copy(sc.at[0, 0, own_rows(k)], g1.at[2, rows(k)], b_s.at[2, k], a_r.at[2, k],
                  chip(across)) for k in range(parts)]
    out_a = [copy(g1s.at[0, rows(k)], g1.at[1, rows(k)], b_s.at[0, k], a_r.at[1, k],
                  chip(outer)) for k in range(parts)]
    out_b = [copy(g1s.at[1, rows(k)], g1.at[2, rows(k)], b_s.at[1, k], a_r.at[2, k],
                  chip(outer)) for k in range(parts)]
    x_near = [copy(sc.at[0, 1, own_rows(k)], g2.at[0, rows(k)], x_s.at[0, k], b_r.at[0, k],
                   chip(near)) for k in range(parts)]
    x_far = [copy(g2s.at[0, rows(k)], g2.at[1, rows(k)], x_s.at[1, k], b_r.at[1, k],
                  chip(across)) for k in range(parts)]
    x_out = [copy(g2s.at[1, rows(k)], g2.at[1, rows(k)], x_s.at[2, k], b_r.at[1, k],
                  chip(outer)) for k in range(parts)]
    steps = [(m, k) for m in range(5) for k in range(parts)]
    u_near, u_far, u_out = {}, {}, {}
    for m, k in steps:
        u_near[m, k] = copy(ars.at[0, m, rows(k)], ar.at[0, m, rows(k)], v_s.at[0, m, k],
                            v_r.at[0, m, k], chip(near))
        u_far[m, k] = copy(ars.at[0, m, rows(k)], ar.at[1, m, rows(k)], v_s.at[0, m, k],
                           v_r.at[1, m, k], chip(across))
        u_out[m, k] = copy(ars.at[1, m, rows(k)], ar.at[1, m, rows(k)], v_s.at[1, m, k],
                           v_r.at[1, m, k], chip(outer))
    sc_to = [copy(sc.at[:, i, own], sc.at[:, i, own], sc_s.at[i], sc_r.at[i], sibling)
             if i else None for i in (0, 1, 2)]
    pt_to = [copy(pt.at[:, i, own], pt.at[:, i, own], pt_s.at[i], pt_r.at[i], sibling)
             for i in range(3)]

    def forward_root(k):
        root_to[k].wait_recv()
        root_on[k].start()

    def relay_one(k):
        @pl.when(is_inner)
        def _():
            a_far[k].wait_recv()
            b_far[k].wait_recv()
            theirs = g1[2, rows(k)].astype(F32)
            g1s[0, rows(k)] = (
                beyond_in * g1[1, rows(k)].astype(F32) + (1.0 - beyond_in) * theirs
            ).astype(BF)
            g1s[1, rows(k)] = (
                near_in * sc[0, 0, own_rows(k)].astype(F32) + (1.0 - near_in) * theirs
            ).astype(BF)
            out_a[k].start()
            out_b[k].start()

    def relay_two(k):
        @pl.when(is_inner)
        def _():
            mine = sc[0, 1, own_rows(k)].astype(F32)
            x_near[k].wait_recv()
            g2s[0, rows(k)] = (g2[0, rows(k)].astype(F32) + mine).astype(BF)
            x_far[k].start()
            x_out[k].wait_recv()
            g2s[1, rows(k)] = (g2[1, rows(k)].astype(F32) + mine).astype(BF)
            x_out[k].start()

    def place(m, k=None):
        at = (m % 2) * half
        return (m // 2, slice(at, at + half) if k is None else slice(at + k * step, at + (k + 1) * step))

    def send_sum(m, value):
        low[place(m)] = value

        @pl.when(is_outer)
        def _():
            ars[0, m] = value.astype(BF)
            for k in range(parts):
                u_near[m, k].start()

    def sum_step(m, k):
        @pl.when(is_inner)
        def _():
            mine = low[place(m, k)]
            u_near[m, k].wait_recv()
            upto = ar[0, m, rows(k)].astype(F32) + mine
            ars[0, m, rows(k)] = upto.astype(BF)
            u_far[m, k].start()
            u_out[m, k].wait_recv()
            rest = ar[1, m, rows(k)].astype(F32)
            ars[1, m, rows(k)] = (rest + mine).astype(BF)
            u_out[m, k].start()
            low[place(m, k)] = upto + rest

        @pl.when(is_outer)
        def _():
            u_out[m, k].wait_recv()
            low[place(m, k)] = low[place(m, k)] + ar[1, m, rows(k)].astype(F32)

    loads["low", 0].wait()
    for _ in inverse_steps(low, inv, 0, starts):
        pass

    def scale(i):
        loads["pf", i].wait()
        pf_to[i].wait_recv()
        value = nt3(both(inv, i, own), split(pf[i])) * kept[i]
        keep(sc, (i, own), value)

    scale(0)

    @pl.when(is_outer)
    def _():
        for k in range(parts):
            a_far[k].start()
            a_near[k].start()

    @pl.when(is_inner)
    def _():
        for k in range(parts):
            b_far[k].start()

    loads["low", 1].wait()
    loads["low", 2].wait()
    events = [functools.partial(forward_root, k) for k in range(3)]
    events += [functools.partial(relay_one, k) for k in range(parts)]
    turn = 0
    for _ in zip(inverse_steps(low, inv, 1, starts), inverse_steps(low, inv, 2, starts)):
        turn += 1
        if turn >= 4 and events:
            events.pop(0)()
    scale(1)

    @pl.when(is_outer)
    def _():
        for k in range(parts):
            x_near[k].start()

    sc_to[1].start()
    scale(2)
    sc_to[2].start()
    for event in events:
        event()

    loads["ch", 0].wait()
    for i in (0, 1):
        keep(ct, (i,), nt3(both(inv, i + 1), split(ch[i])))
    relay_two(0)
    for i in range(3):
        gram[i] = nt3(both(inv, i, own), both(inv, i))
        if i:
            relay_two(i)

    loads["root", 0].wait()
    root_own.wait_recv()
    for k in range(3):
        root_on[k].wait_recv()
    acc[...] = nt(sc[0, 0, own], root[z])

    @pl.when(is_inner)
    def _():
        for k in range(parts):
            a_near[k].wait_recv()
        acc[...] += nt(g1[0], root[outer])

    @pl.when(is_outer)
    def _():
        for k in range(parts):
            out_a[k].wait_recv()
            out_b[k].wait_recv()

    acc[...] += nt(g1[1], root[a_index]) + nt(g1[2], root[b_index])
    first_panel = acc[...] * -kept[0]
    keep(pt, (0, own), first_panel)
    pt_to[0].start()
    sc_to[1].wait_recv()
    sc_to[2].wait_recv()
    send_sum(0, nt3(both(pt, 0, own), both(sc, 1)))
    pt_to[0].wait_recv()
    send_sum(1, nt3(both(sc, 0, own), both(pt, 0)))

    @pl.when(is_outer)
    def _():
        for k in range(parts):
            x_out[k].wait_recv()
        g2[0] = g2[1]

    @pl.when(is_inner)
    def _():
        g2[0] = (g2[0].astype(F32) + g2[1].astype(F32)).astype(BF)

    value = nt(sc[0, 1, own], root[z]) + nt(g2[0], root[other_index])
    value = (value + dot3(both(ct, 0, own), both(pt, 0))) * -kept[1]
    keep(pt, (1, own), value)
    pt_to[1].start()
    send_sum(2, nt3(both(pt, 1, own), both(sc, 2)))
    for k in range(parts):
        sum_step(0, k)
    pt_to[1].wait_recv()
    send_sum(3, nt3(both(sc, 1, own), both(pt, 1)))
    for k in range(parts):
        sum_step(1, k)

    value = nt(sc[0, 2, own], root[z])
    value = (value + dot3(both(ct, 1, own), both(pt, 1))) * -kept[2]
    keep(pt, (2, own), value)
    pt_to[2].start()

    def give(index, value, sem):
        block_out[0, index, own] = value
        block = block_out.at[0, index, own]
        return copy(block, block, out_s.at[sem], out_r.at[sem], sibling)

    gives = {}
    pt_to[2].wait_recv()
    send_sum(4, nt3(both(sc, 2, own), both(pt, 2)))
    gives[0] = give(0, gram[0] - low[place(1)], 0)
    gives[0].start()
    known = split(block_out[0, 0, own])
    gives[3] = give(3, -(low[place(0)] + nt3(known, both(ct, 0))), 3)
    gives[3].start()
    for k in range(parts):
        sum_step(2, k)

    pick = jnp.where(
        lax.broadcasted_iota(jnp.int32, (half, size), 1)
        == lax.broadcasted_iota(jnp.int32, (half, size), 0) + core * half,
        1.0, 0.0,
    ).astype(BF)
    for i in range(3):
        panel_out[0, i] = nt(pick, pt[0, i]) + nt(pick, pt[1, i])
    for k in range(parts):
        sum_step(3, k)
    gives[3].wait_recv()
    value = gram[1] - low[place(3)] - dot3(both(ct, 0, own), split(block_out[0, 3]))
    gives[1] = give(1, value, 1)
    gives[1].start()
    gives[4] = give(4, -(low[place(2)] + nt3(split(value), both(ct, 1))), 4)
    gives[4].start()
    gives[4].wait_recv()
    gram[2] = gram[2] - dot3(both(ct, 1, own), split(block_out[0, 4]))
    for k in range(parts):
        sum_step(4, k)
        at = own_rows(k)
        block_out[0, 2, at] = gram[2, rows(k)] - low[place(4, k)]
        block = block_out.at[0, 2, at]
        gives[5 + k] = copy(block, block, out_s.at[5 + k], out_r.at[5 + k], sibling)
        gives[5 + k].start()
    for i in (0, 1):
        gives[i].wait_recv()
    for k in range(parts):
        gives[5 + k].wait_recv()

    for one in [*pf_to, *root_to, root_own, *root_on, sc_to[1], sc_to[2], *pt_to, *gives.values()]:
        one.wait_send()

    @pl.when(is_outer)
    def _():
        for one in [*a_far, *a_near, *x_near, *u_near.values()]:
            one.wait_send()

    @pl.when(is_inner)
    def _():
        for one in [*b_far, *out_a, *out_b, *x_far, *x_out, *u_far.values(), *u_out.values()]:
            one.wait_send()


def whole(root_cov, diag_factor, panel_factor, chain_factor, panel_tiles):
    size = diag_factor.shape[-1]
    half = size // 2
    dma = pltpu.SemaphoreType.DMA
    anywhere = pl.BlockSpec(memory_space=pl.ANY)
    inside = pl.BlockSpec(memory_space=pltpu.VMEM)
    vm = pltpu.VMEM
    return pl.pallas_call(
        functools.partial(whole_kernel, size),
        out_shape=(
            jax.ShapeDtypeStruct((1, 3, half, size), F32),
            jax.ShapeDtypeStruct((1, 5, size, size), F32),
        ),
        in_specs=[pl.BlockSpec(memory_space=pltpu.SMEM)] + [anywhere] * 4,
        out_specs=(inside, inside),
        scratch_shapes=[
            vm((3, size, size), F32),
            vm((3, size, size), F32),
            vm((2, size, size), F32),
            vm((4, size, size), BF),
            vm((2, 3, size, size), BF),
            vm((2, 3, size, size), BF),
            vm((2, 2, size, size), BF),
            vm((2, 3, size, size), BF),
            vm((half, size), F32),
            vm((3, half, size), F32),
            vm((3, half, size), BF),
            vm((2, half, size), BF),
            vm((2, half, size), BF),
            vm((2, half, size), BF),
            vm((2, 5, half, size), BF),
            vm((2, 5, half, size), BF),
            dma((8,)), dma((3,)), dma((3,)), dma((3,)), dma((3,)), dma((4,)), dma((4,)),
            dma((3,)), dma((3,)), dma((3,)), dma((3,)),
            dma((2, 3)), dma((3, 3)), dma((3, 3)), dma((2, 3)),
            dma((3, 3)), dma((2, 5, 3)), dma((2, 5, 3)), dma((8,)), dma((8,)),
        ],
        compiler_params=pltpu.CompilerParams(
            collective_id=0, has_side_effects=True, vmem_limit_bytes=60 * 2**20
        ),
        name="whole",
    )(panel_tiles, root_cov, diag_factor, panel_factor, chain_factor)


def on_device(root_cov, diag_factor, panel_factor, chain_factor, panel_tiles):
    node_width = diag_factor.shape[-1]
    rows_here = panel_factor.shape[2]
    per_tile = node_width // rows_here
    row_count = lax.axis_size("row")
    tile_total = row_count // per_tile
    counts = (3 * tile_total // 4, tile_total // 2, tile_total // 4)
    small = row_count == 8 and tile_total == 4 and root_cov.shape[1] == node_width
    if small:
        return whole(root_cov, diag_factor, panel_factor, chain_factor, panel_tiles)
    root_rows = lax.all_gather(root_cov, "branch", axis=1, tiled=True)
    me = lax.axis_index("row")
    my_tile = me // per_tile
    inverse_all = inverses(diag_factor)
    share = -(-node_width // row_count // 8) * 8
    padded = jnp.pad(inverse_all, ((0, 0), (0, share * row_count - node_width), (0, 0)))
    mine = lax.dynamic_slice_in_dim(padded, me * share, share, axis=1)
    chosen = [jnp.any(panel_tiles[0, : counts[i]] == my_tile) for i in range(3)]
    scaled = [
        jnp.where(chosen[i], product(panel_factor[0, i], inverse_all[i]), 0.0) for i in range(3)
    ]
    panels = []
    blocks = []
    crosses = []
    for i in range(3):
        rounded = scaled[i].astype(BF)
        gathered = jnp.dot(
            root_rows,
            lax.all_gather(rounded, "row", axis=0, tiled=True),
            preferred_element_type=F32,
        )
        left = jnp.concatenate([mine[i], scaled[i]], axis=0)
        if i == 0:
            panel = -jnp.where(chosen[i], gathered, 0.0)
            block = product(left.T, jnp.concatenate([mine[i], -panel], axis=0))
        else:
            chain = product(chain_factor[0, i - 1], inverse_all[i])
            panel = -jnp.where(chosen[i], gathered + product(panels[-1], chain), 0.0)
            cross = -(product(panels[-1].T, scaled[i]) + product(blocks[-1], chain))
            block = product(left.T, jnp.concatenate([mine[i], -panel], axis=0)) - product(
                chain.T, cross
            )
            crosses.append(cross)
        panels.append(panel)
        blocks.append(block)
    total = lax.psum(jnp.stack(blocks + crosses), "row")
    return (jnp.stack(panels)[None], total[None])


def solution(mesh):
    in_specs = (
        P("row", "branch"),
        P("branch", None, None, None),
        P("branch", None, "row", None),
        P("branch", None, None, None),
        P("branch", None),
    )
    out_specs = (P("branch", None, "row", None), P("branch", None, None, None))
    return jax.shard_map(
        on_device, mesh=mesh, in_specs=in_specs, out_specs=out_specs, check_vma=False
    )
```

```python
import functools
import jax
import jax.numpy as jnp
from jax import lax
from jax.experimental import pallas as pl
from jax.experimental.pallas import tpu as pltpu
from jax.sharding import PartitionSpec as P

BF = jnp.bfloat16
F32 = jnp.float32
MESH = pl.DeviceIdType.MESH


def product(left_mat, right_mat):
    return jnp.dot(left_mat, right_mat, precision=lax.Precision.HIGH, preferred_element_type=F32)


def split(x):
    hi = x.astype(BF)
    return hi, (x - hi.astype(F32)).astype(BF)


def mm(a, b):
    return jnp.dot(a, b, preferred_element_type=F32)


def dot3(a, b):
    a_hi, a_lo = a
    b_hi, b_lo = b
    return mm(a_hi, b_hi) + (mm(a_lo, b_hi) + mm(a_hi, b_lo))


def inverse_kernel(size, window, l_ref, out_ref):
    count = size // window
    row = lax.broadcasted_iota(jnp.int32, (window, window), 0)
    col = lax.broadcasted_iota(jnp.int32, (window, window), 1)
    eye = row == col
    diagonals = []
    for w in range(count):
        at = slice(w * window, (w + 1) * window)
        block = l_ref[0, 0, at, at]
        kept = jnp.where(eye, block, 0.0)
        down = 1.0 / jnp.sum(kept, axis=1, keepdims=True)
        across = 1.0 / jnp.sum(kept, axis=0, keepdims=True)
        diagonals.append((block * down, across))
    found = []
    for scaled, across in diagonals:
        x = jnp.where(eye, 1.0, 0.0)
        x = x - jnp.where((row // 2 == col // 2) & (row > col), scaled, 0.0)
        found.append(x)
    k = 2
    while k < window:
        pair = (row // (2 * k) == col // (2 * k)) & (row // k > col // k)
        for w in range(count):
            x = found[w]
            parts = split(x)
            right = dot3(split(jnp.where(pair, diagonals[w][0], 0.0)), parts)
            found[w] = x - dot3(parts, split(right))
        k *= 2
    found = [x * diagonals[w][1] for w, x in enumerate(found)]
    done = {}
    for w in range(count):
        done[w, w] = split(found[w])
        out_ref[0, w * window:(w + 1) * window, w * window:(w + 1) * window] = found[w]
    for gap in range(1, count):
        for c in range(count - gap):
            r = c + gap
            total = None
            for m in range(c, r):
                below = split(l_ref[0, 0, r * window:(r + 1) * window, m * window:(m + 1) * window])
                term = dot3(below, done[m, c])
                total = term if total is None else total + term
            value = -dot3(done[r, r], split(total))
            done[r, c] = split(value)
            out_ref[0, r * window:(r + 1) * window, c * window:(c + 1) * window] = value
            out_ref[0, c * window:(c + 1) * window, r * window:(r + 1) * window] = jnp.zeros(
                (window, window), F32
            )


def inverses(diag_factor):
    levels, size = diag_factor.shape[1], diag_factor.shape[-1]
    return pl.pallas_call(
        functools.partial(inverse_kernel, size, size // 3),
        grid=(levels,),
        in_specs=[pl.BlockSpec((1, 1, size, size), lambda i: (0, i, 0, 0))],
        out_specs=pl.BlockSpec((1, size, size), lambda i: (i, 0, 0)),
        out_shape=jax.ShapeDtypeStruct((levels, size, size), F32),
        compiler_params=pltpu.CompilerParams(vmem_limit_bytes=48 * 2**20),
        name="inverses",
    )(diag_factor)


def nt(a, b):
    return lax.dot_general(a, b, (((1,), (1,)), ((), ())), preferred_element_type=F32)


def nt3(a, b):
    return nt(a[0], b[0]) + (nt(a[1], b[0]) + nt(a[0], b[1]))


def inverse_steps(low, inv, level, starts):
    found, scaled, downs, pairs, eyes = [], [], [], [], []
    for at, to in starts:
        span = to - at
        row = lax.broadcasted_iota(jnp.int32, (span, span), 0)
        col = lax.broadcasted_iota(jnp.int32, (span, span), 1)
        eye = row == col
        block = low[level, at:to, at:to]
        down = 1.0 / jnp.sum(jnp.where(eye, block, 0.0), axis=1, keepdims=True)
        scaled.append(jnp.where(row > col, block * down, 0.0))
        downs.append(down)
        pairs.append(row ^ col)
        eyes.append(jnp.where(eye, 1.0, 0.0))
        first = split(jnp.where(pairs[-1] == 1, scaled[-1], 0.0))
        unit = eyes[-1].astype(BF)
        found.append(eyes[-1] - (nt(unit, first[0]) + nt(unit, first[1])))
    yield
    k = 2
    while k < starts[0][1] - starts[0][0]:
        for w, (at, to) in enumerate(starts):
            if k < to - at:
                parts = split(found[w])
                pair = (pairs[w] >= k) & (pairs[w] < 2 * k)
                right = nt3(parts, split(jnp.where(pair, scaled[w], 0.0)))
                found[w] = found[w] - dot3(split(right), parts)
        k *= 2
        yield
    done = {}

    def keep(c, r, value):
        done[c, r] = split(value)
        rows, columns = slice(*starts[c]), slice(*starts[r])
        inv[0, level, rows, columns] = done[c, r][0]
        inv[1, level, rows, columns] = done[c, r][1]

    for w in range(len(starts)):
        keep(w, w, found[w] * downs[w])
    for gap in range(1, len(starts)):
        for c in range(len(starts) - gap):
            r = c + gap
            total = None
            for m in range(c, r):
                below = split(low[level, slice(*starts[r]), slice(*starts[m])])
                term = nt3(done[c, m], below)
                total = term if total is None else total + term
            keep(c, r, -dot3(split(total), done[r, r]))
            zero = jnp.zeros((starts[r][1] - starts[r][0], starts[c][1] - starts[c][0]), BF)
            inv[0, level, slice(*starts[r]), slice(*starts[c])] = zero
            inv[1, level, slice(*starts[r]), slice(*starts[c])] = zero
        yield


def pack(x):
    rows, columns = x.shape
    full = columns // 128 * 128
    pieces = [x[:, at:at + 128] for at in range(0, full, 128)]
    rest = jnp.concatenate([x[:rows // 2, full:], x[rows // 2:, full:]], axis=1)
    return jnp.concatenate([*pieces, rest], axis=0)


def unpack(x, columns):
    rows = x.shape[0] * 128 // columns
    full = columns // 128
    pieces = [x[i * rows:(i + 1) * rows] for i in range(full)]
    rest = x[full * rows:]
    return jnp.concatenate(
        [*pieces, jnp.concatenate([rest[:, :64], rest[:, 64:]], axis=0)], axis=1
    )


def whole_kernel(size, parts, tiles, root_in, low_in, panel_in, chain_in, panel_out, block_out,
                 low, pf, ch, root, inv, sc, ct, pt, acc, gram, own_sum, sp, g1, g1s, g2, g2s, ar, ars,
                 load_s, pf_s, pf_r, root_s, root_r, fwd_s, fwd_r, sc_s, sc_r, pt_s, pt_r,
                 a_s, a_r, b_s, b_r, x_s, v_s, v_r, out_s, out_r):
    half = size // 2
    step = half // parts
    packed = step * size // 128
    branch = lax.axis_index("branch")
    me = lax.axis_index("row")
    z = me // 2
    core = me % 2
    side = z // 2
    outer, near, across, beyond = 3 * side, 1 + side, 2 - side, 3 - 3 * side
    is_inner = z == near
    is_outer = z == outer
    own = pl.ds(pl.multiple_of(core * half, 32), half)
    sibling = {"row": 2 * z + 1 - core}

    def chip(at):
        return {"row": 2 * at + core}

    def copy(src, dst, send_sem, recv_sem, target):
        return pltpu.make_async_remote_copy(
            src_ref=src, dst_ref=dst, send_sem=send_sem, recv_sem=recv_sem,
            device_id=target, device_id_type=MESH,
        )

    barrier = pltpu.get_barrier_semaphore()
    peers = [sibling] + [chip((z + k) % 4) for k in (1, 2, 3)]
    peers += [{"branch": (branch + k) % 4} for k in (1, 2, 3)]
    for peer in peers:
        pl.semaphore_signal(barrier, inc=1, device_id=peer, device_id_type=MESH)

    loads = {}
    for i in range(3):
        loads["low", i] = pltpu.make_async_copy(low_in.at[0, i], low.at[i], load_s.at[i])
        loads["pf", i] = pltpu.make_async_copy(
            panel_in.at[0, i], pf.at[i, own], load_s.at[3 + i]
        )
    loads["ch", 0] = pltpu.make_async_copy(chain_in.at[0], ch, load_s.at[6])
    loads["root", 0] = pltpu.make_async_copy(root_in, root.at[branch, own], load_s.at[7])
    for key in (("low", 0), ("pf", 0), ("root", 0), ("low", 1), ("low", 2), ("pf", 1), ("pf", 2),
                ("ch", 0)):
        loads[key].start()
    pl.semaphore_wait(barrier, 7)

    pf_to = [
        copy(panel_in.at[0, i], pf.at[i, own], pf_s.at[i], pf_r.at[i], sibling) for i in range(3)
    ]
    root_to = [
        copy(root_in, root.at[branch, own], root_s.at[k - 1], root_r.at[k - 1],
             {"branch": (branch + k) % 4})
        for k in (1, 2, 3)
    ]
    root_own = copy(root_in, root.at[branch, own], fwd_s.at[0], fwd_r.at[0], sibling)
    root_on = []
    for k in (1, 2, 3):
        block = root.at[(branch + 4 - k) % 4, own]
        root_on.append(copy(block, block, fwd_s.at[k], fwd_r.at[k], sibling))
    pf_to[0].start()
    for k in range(3):
        root_to[k].start()
    root_own.start()
    pf_to[1].start()
    pf_to[2].start()

    first, second, third = tiles[0, 0], tiles[0, 1], tiles[0, 2]

    def among(tile, count):
        hit = tile == first
        if count > 1:
            hit = hit | (tile == second)
        if count > 2:
            hit = hit | (tile == third)
        return jnp.where(hit, 1.0, 0.0)

    kept = [among(z, 3), among(z, 2), among(z, 1)]
    near_in, beyond_in = among(near, 3), among(beyond, 3)
    a_index = jnp.where(is_outer & (beyond_in < 0.5), across, beyond)
    b_index = jnp.where(is_outer & (near_in > 0.5), near, across)
    other_index = jnp.where(z == first, second, first)

    bounds = list(range(0, size, 256)) + [size]
    starts = list(zip(bounds[:-1], bounds[1:]))

    def rows(k):
        return slice(k * packed, (k + 1) * packed)

    def own_rows(k):
        return pl.ds(pl.multiple_of(core * half + k * step, 32), step)

    def cut(value, k):
        return value[k * step:(k + 1) * step]

    def whole_of(ref, *index):
        return jnp.concatenate(
            [unpack(ref[(*index, rows(k))].astype(F32), size) for k in range(parts)], axis=0
        )

    def both(ref, *index):
        return ref[(0, *index)], ref[(1, *index)]

    def keep(ref, index, value):
        hi, lo = split(value)
        ref[(0, *index)] = hi
        ref[(1, *index)] = lo

    a_far = [copy(sp.at[0, rows(k)], g1.at[1, rows(k)], a_s.at[0, k], a_r.at[1, k],
                  chip(across)) for k in range(parts)]
    a_near = [copy(sp.at[0, rows(k)], g1.at[0, rows(k)], a_s.at[1, k], a_r.at[0, k],
                   chip(near)) for k in range(parts)]
    b_far = [copy(sp.at[0, rows(k)], g1.at[2, rows(k)], b_s.at[2, k], a_r.at[2, k],
                  chip(across)) for k in range(parts)]
    out_a = [copy(g1s.at[0, rows(k)], g1.at[1, rows(k)], b_s.at[0, k], a_r.at[1, k],
                  chip(outer)) for k in range(parts)]
    out_b = [copy(g1s.at[1, rows(k)], g1.at[2, rows(k)], b_s.at[1, k], a_r.at[2, k],
                  chip(outer)) for k in range(parts)]
    x_near = [copy(sp.at[1, rows(k)], g2.at[0, rows(k)], x_s.at[0, k], b_r.at[0, k],
                   chip(near)) for k in range(parts)]
    x_far = [copy(g2s.at[0, rows(k)], g2.at[1, rows(k)], x_s.at[1, k], b_r.at[1, k],
                  chip(across)) for k in range(parts)]
    x_out = [copy(g2s.at[1, rows(k)], g2.at[1, rows(k)], x_s.at[2, k], b_r.at[1, k],
                  chip(outer)) for k in range(parts)]
    steps = [(m, k) for m in range(5) for k in range(parts)]
    u_near, u_far, u_out = {}, {}, {}
    for m, k in steps:
        u_near[m, k] = copy(ars.at[0, m, rows(k)], ar.at[0, m, rows(k)], v_s.at[0, m, k],
                            v_r.at[0, m, k], chip(near))
        u_far[m, k] = copy(ars.at[0, m, rows(k)], ar.at[1, m, rows(k)], v_s.at[0, m, k],
                           v_r.at[1, m, k], chip(across))
        u_out[m, k] = copy(ars.at[1, m, rows(k)], ar.at[1, m, rows(k)], v_s.at[1, m, k],
                           v_r.at[1, m, k], chip(outer))
    sc_to = [copy(sc.at[:, i, own], sc.at[:, i, own], sc_s.at[i], sc_r.at[i], sibling)
             if i else None for i in (0, 1, 2)]
    pt_to = [copy(pt.at[:, i, own], pt.at[:, i, own], pt_s.at[i], pt_r.at[i], sibling)
             for i in range(3)]

    def forward_root(k):
        root_to[k].wait_recv()
        root_on[k].start()

    def relay_one(k):
        @pl.when(is_inner)
        def _():
            a_far[k].wait_recv()
            b_far[k].wait_recv()
            theirs = g1[2, rows(k)].astype(F32)
            g1s[0, rows(k)] = (
                beyond_in * g1[1, rows(k)].astype(F32) + (1.0 - beyond_in) * theirs
            ).astype(BF)
            g1s[1, rows(k)] = (
                near_in * sp[0, rows(k)].astype(F32) + (1.0 - near_in) * theirs
            ).astype(BF)
            out_a[k].start()
            out_b[k].start()

    def near_two(k):
        @pl.when(is_inner)
        def _():
            x_near[k].wait_recv()
            mine = sp[1, rows(k)].astype(F32)
            g2s[0, rows(k)] = (g2[0, rows(k)].astype(F32) + mine).astype(BF)
            x_far[k].start()

    def far_two(k):
        @pl.when(is_inner)
        def _():
            x_out[k].wait_recv()
            mine = sp[1, rows(k)].astype(F32)
            g2s[1, rows(k)] = (g2[1, rows(k)].astype(F32) + mine).astype(BF)
            x_out[k].start()

    def send_sum(m, value):
        for k in range(parts):
            mine = pack(cut(value, k))
            own_sum[m, rows(k)] = mine
            ars[0, m, rows(k)] = mine.astype(BF)

        @pl.when(is_outer)
        def _():
            for k in range(parts):
                u_near[m, k].start()

    def near_sum(m, k):
        @pl.when(is_inner)
        def _():
            u_near[m, k].wait_recv()
            upto = ar[0, m, rows(k)].astype(F32) + own_sum[m, rows(k)]
            ars[0, m, rows(k)] = upto.astype(BF)
            u_far[m, k].start()

    def far_sum(m, k):
        @pl.when(is_inner)
        def _():
            u_out[m, k].wait_recv()
            rest = ar[1, m, rows(k)].astype(F32) + own_sum[m, rows(k)]
            ars[1, m, rows(k)] = rest.astype(BF)
            u_out[m, k].start()
            own_sum[m, rows(k)] = rest + ar[0, m, rows(k)].astype(F32)

        @pl.when(is_outer)
        def _():
            u_out[m, k].wait_recv()
            own_sum[m, rows(k)] = own_sum[m, rows(k)] + ar[1, m, rows(k)].astype(F32)

    lag = 1
    order = []
    for i in range(len(steps) + lag):
        if i < len(steps):
            order.append(functools.partial(near_sum, *steps[i]))
        if i >= lag:
            order.append(functools.partial(far_sum, *steps[i - lag]))
    done = [0]

    def pump(until):
        stop = min(2 * until + 2 + lag, len(order))
        while done[0] < stop:
            order[done[0]]()
            done[0] += 1

    loads["low", 0].wait()
    for _ in inverse_steps(low, inv, 0, starts):
        pass

    def scale(i):
        loads["pf", i].wait()
        pf_to[i].wait_recv()
        value = nt3(both(inv, i, own), split(pf[i])) * kept[i]
        keep(sc, (i, own), value)
        if i < 2:
            for k in range(parts):
                sp[i, rows(k)] = pack(cut(value, k)).astype(BF)

    scale(0)

    @pl.when(is_outer)
    def _():
        for k in range(parts):
            a_far[k].start()
            a_near[k].start()

    @pl.when(is_inner)
    def _():
        for k in range(parts):
            b_far[k].start()

    loads["low", 1].wait()
    loads["low", 2].wait()
    events = {5: [functools.partial(forward_root, k) for k in range(3)]}
    events[8] = [functools.partial(relay_one, 0)]
    turn = 0
    for _ in zip(inverse_steps(low, inv, 1, starts), inverse_steps(low, inv, 2, starts)):
        turn += 1
        for event in events.get(turn, ()):
            event()
    scale(1)

    @pl.when(is_outer)
    def _():
        for k in range(parts):
            x_near[k].start()

    sc_to[1].start()
    relay_one(1)
    scale(2)
    sc_to[2].start()
    loads["ch", 0].wait()
    keep(ct, (0,), nt3(both(inv, 1), split(ch[0])))
    for k in range(2, parts):
        relay_one(k)
    keep(ct, (1,), nt3(both(inv, 2), split(ch[1])))
    gram[0] = nt3(both(inv, 0, own), both(inv, 0))
    near_two(0)
    gram[1] = nt3(both(inv, 1, own), both(inv, 1))
    near_two(1)
    far_two(0)
    gram[2] = nt3(both(inv, 2, own), both(inv, 2))
    loads["root", 0].wait()
    root_own.wait_recv()
    for k in range(3):
        root_on[k].wait_recv()
    acc[...] = nt(sc[0, 0, own], root[z])

    @pl.when(is_inner)
    def _():
        for k in range(parts):
            a_near[k].wait_recv()
        acc[...] += nt(whole_of(g1, 0).astype(BF), root[outer])

    @pl.when(is_outer)
    def _():
        for k in range(parts):
            out_a[k].wait_recv()
            out_b[k].wait_recv()

    acc[...] += nt(whole_of(g1, 1).astype(BF), root[a_index])
    acc[...] += nt(whole_of(g1, 2).astype(BF), root[b_index])
    first_panel = acc[...] * -kept[0]
    keep(pt, (0, own), first_panel)
    pt_to[0].start()
    sc_to[1].wait_recv()
    sc_to[2].wait_recv()
    send_sum(0, nt3(both(pt, 0, own), both(sc, 1)))
    pt_to[0].wait_recv()
    send_sum(1, nt3(both(sc, 0, own), both(pt, 0)))

    for k in range(2, parts + 1):
        if k < parts:
            near_two(k)
        far_two(k - 1)

    @pl.when(is_outer)
    def _():
        for k in range(parts):
            x_out[k].wait_recv()
        acc[...] = whole_of(g2, 1)

    @pl.when(is_inner)
    def _():
        acc[...] = whole_of(g2, 0) + whole_of(g2, 1)

    value = nt(sc[0, 1, own], root[z]) + nt(acc[...].astype(BF), root[other_index])
    value = (value + dot3(both(ct, 0, own), both(pt, 0))) * -kept[1]
    keep(pt, (1, own), value)
    pt_to[1].start()
    send_sum(2, nt3(both(pt, 1, own), both(sc, 2)))
    pump(0)
    pt_to[1].wait_recv()
    send_sum(3, nt3(both(sc, 1, own), both(pt, 1)))
    pump(1)

    value = nt(sc[0, 2, own], root[z])
    value = (value + dot3(both(ct, 1, own), both(pt, 1))) * -kept[2]
    keep(pt, (2, own), value)
    pt_to[2].start()
    pump(2)

    def give(index, value, sem):
        block_out[0, index, own] = value
        block = block_out.at[0, index, own]
        return copy(block, block, out_s.at[sem], out_r.at[sem], sibling)

    gives = {}
    pt_to[2].wait_recv()
    send_sum(4, nt3(both(sc, 2, own), both(pt, 2)))
    pump(2 * parts - 1)
    gives[0] = give(0, gram[0] - whole_of(own_sum, 1), 0)
    gives[0].start()
    known = split(block_out[0, 0, own])
    gives[3] = give(3, -(whole_of(own_sum, 0) + nt3(known, both(ct, 0))), 3)
    gives[3].start()
    pump(2 * parts)

    pick = jnp.where(
        lax.broadcasted_iota(jnp.int32, (half, size), 1)
        == lax.broadcasted_iota(jnp.int32, (half, size), 0) + core * half,
        1.0, 0.0,
    ).astype(BF)
    for i in range(3):
        panel_out[0, i] = nt(pick, pt[0, i]) + nt(pick, pt[1, i])
        pump(2 * parts + 1 + i)
    pump(4 * parts - 1)
    gives[3].wait_recv()
    value = gram[1] - whole_of(own_sum, 3) - dot3(both(ct, 0, own), split(block_out[0, 3]))
    gives[1] = give(1, value, 1)
    gives[1].start()
    gives[4] = give(4, -(whole_of(own_sum, 2) + nt3(split(value), both(ct, 1))), 4)
    gives[4].start()
    gives[4].wait_recv()
    gram[2] = gram[2] - dot3(both(ct, 1, own), split(block_out[0, 4]))
    for k in range(parts):
        pump(4 * parts + k)
        at = own_rows(k)
        block_out[0, 2, at] = gram[2, k * step:(k + 1) * step] - unpack(own_sum[4, rows(k)], size)
        block = block_out.at[0, 2, at]
        gives[5 + k] = copy(block, block, out_s.at[5 + k], out_r.at[5 + k], sibling)
        gives[5 + k].start()
    for i in (0, 1):
        gives[i].wait_recv()
    for k in range(parts):
        gives[5 + k].wait_recv()

    for one in [*pf_to, *root_to, root_own, *root_on, sc_to[1], sc_to[2], *pt_to, *gives.values()]:
        one.wait_send()

    @pl.when(is_outer)
    def _():
        for one in [*a_far, *a_near, *x_near, *u_near.values()]:
            one.wait_send()

    @pl.when(is_inner)
    def _():
        for one in [*b_far, *out_a, *out_b, *x_far, *x_out, *u_far.values(), *u_out.values()]:
            one.wait_send()


def whole(root_cov, diag_factor, panel_factor, chain_factor, panel_tiles):
    size = diag_factor.shape[-1]
    half = size // 2
    parts = 3
    line = half * size // 128
    dma = pltpu.SemaphoreType.DMA
    anywhere = pl.BlockSpec(memory_space=pl.ANY)
    inside = pl.BlockSpec(memory_space=pltpu.VMEM)
    vm = pltpu.VMEM
    return pl.pallas_call(
        functools.partial(whole_kernel, size, parts),
        out_shape=(vm((1, 3, half, size), F32), vm((1, 5, size, size), F32)),
        in_specs=[pl.BlockSpec(memory_space=pltpu.SMEM)] + [anywhere] * 4,
        out_specs=(inside, inside),
        scratch_shapes=[
            vm((3, size, size), F32),
            vm((3, size, size), F32),
            vm((2, size, size), F32),
            vm((4, size, size), BF),
            vm((2, 3, size, size), BF),
            vm((2, 3, size, size), BF),
            vm((2, 2, size, size), BF),
            vm((2, 3, size, size), BF),
            vm((half, size), F32),
            vm((3, half, size), F32),
            vm((5, line, 128), F32),
            vm((2, line, 128), BF),
            vm((3, line, 128), BF),
            vm((2, line, 128), BF),
            vm((2, line, 128), BF),
            vm((2, line, 128), BF),
            vm((2, 5, line, 128), BF),
            vm((2, 5, line, 128), BF),
            dma((8,)), dma((3,)), dma((3,)), dma((3,)), dma((3,)), dma((4,)), dma((4,)),
            dma((3,)), dma((3,)), dma((3,)), dma((3,)),
            dma((2, parts)), dma((3, parts)), dma((3, parts)), dma((2, parts)),
            dma((3, parts)), dma((2, 5, parts)), dma((2, 5, parts)), dma((5 + parts,)),
            dma((5 + parts,)),
        ],
        compiler_params=pltpu.CompilerParams(
            collective_id=0, has_side_effects=True, vmem_limit_bytes=52 * 2**20
        ),
        name="whole",
    )(panel_tiles, root_cov, diag_factor, panel_factor, chain_factor)


def on_device(root_cov, diag_factor, panel_factor, chain_factor, panel_tiles):
    node_width = diag_factor.shape[-1]
    rows_here = panel_factor.shape[2]
    per_tile = node_width // rows_here
    row_count = lax.axis_size("row")
    tile_total = row_count // per_tile
    counts = (3 * tile_total // 4, tile_total // 2, tile_total // 4)
    small = row_count == 8 and tile_total == 4 and root_cov.shape[1] == node_width
    if small:
        return whole(root_cov, diag_factor, panel_factor, chain_factor, panel_tiles)
    root_rows = lax.all_gather(root_cov, "branch", axis=1, tiled=True)
    me = lax.axis_index("row")
    my_tile = me // per_tile
    inverse_all = inverses(diag_factor)
    share = -(-node_width // row_count // 8) * 8
    padded = jnp.pad(inverse_all, ((0, 0), (0, share * row_count - node_width), (0, 0)))
    mine = lax.dynamic_slice_in_dim(padded, me * share, share, axis=1)
    chosen = [jnp.any(panel_tiles[0, : counts[i]] == my_tile) for i in range(3)]
    scaled = [
        jnp.where(chosen[i], product(panel_factor[0, i], inverse_all[i]), 0.0) for i in range(3)
    ]
    panels = []
    blocks = []
    crosses = []
    for i in range(3):
        rounded = scaled[i].astype(BF)
        gathered = jnp.dot(
            root_rows,
            lax.all_gather(rounded, "row", axis=0, tiled=True),
            preferred_element_type=F32,
        )
        left = jnp.concatenate([mine[i], scaled[i]], axis=0)
        if i == 0:
            panel = -jnp.where(chosen[i], gathered, 0.0)
            block = product(left.T, jnp.concatenate([mine[i], -panel], axis=0))
        else:
            chain = product(chain_factor[0, i - 1], inverse_all[i])
            panel = -jnp.where(chosen[i], gathered + product(panels[-1], chain), 0.0)
            cross = -(product(panels[-1].T, scaled[i]) + product(blocks[-1], chain))
            block = product(left.T, jnp.concatenate([mine[i], -panel], axis=0)) - product(
                chain.T, cross
            )
            crosses.append(cross)
        panels.append(panel)
        blocks.append(block)
    total = lax.psum(jnp.stack(blocks + crosses), "row")
    return (jnp.stack(panels)[None], total[None])


def solution(mesh):
    in_specs = (
        P("row", "branch"),
        P("branch", None, None, None),
        P("branch", None, "row", None),
        P("branch", None, None, None),
        P("branch", None),
    )
    out_specs = (P("branch", None, "row", None), P("branch", None, None, None))
    return jax.shard_map(
        on_device, mesh=mesh, in_specs=in_specs, out_specs=out_specs, check_vma=False
    )
```

```python
import functools
import jax
import jax.numpy as jnp
from jax import lax
from jax.experimental import pallas as pl
from jax.experimental.pallas import tpu as pltpu
from jax.sharding import PartitionSpec as P

BF = jnp.bfloat16
F32 = jnp.float32
MESH = pl.DeviceIdType.MESH


def product(left_mat, right_mat):
    return jnp.dot(left_mat, right_mat, precision=lax.Precision.HIGH, preferred_element_type=F32)


def split(x):
    hi = x.astype(BF)
    return hi, (x - hi.astype(F32)).astype(BF)


def mm(a, b):
    return jnp.dot(a, b, preferred_element_type=F32)


def dot3(a, b):
    a_hi, a_lo = a
    b_hi, b_lo = b
    return mm(a_hi, b_hi) + (mm(a_lo, b_hi) + mm(a_hi, b_lo))


def inverse_kernel(size, window, l_ref, out_ref):
    count = size // window
    row = lax.broadcasted_iota(jnp.int32, (window, window), 0)
    col = lax.broadcasted_iota(jnp.int32, (window, window), 1)
    eye = row == col
    diagonals = []
    for w in range(count):
        at = slice(w * window, (w + 1) * window)
        block = l_ref[0, 0, at, at]
        kept = jnp.where(eye, block, 0.0)
        down = 1.0 / jnp.sum(kept, axis=1, keepdims=True)
        across = 1.0 / jnp.sum(kept, axis=0, keepdims=True)
        diagonals.append((block * down, across))
    found = []
    for scaled, across in diagonals:
        x = jnp.where(eye, 1.0, 0.0)
        x = x - jnp.where((row // 2 == col // 2) & (row > col), scaled, 0.0)
        found.append(x)
    k = 2
    while k < window:
        pair = (row // (2 * k) == col // (2 * k)) & (row // k > col // k)
        for w in range(count):
            x = found[w]
            parts = split(x)
            right = dot3(split(jnp.where(pair, diagonals[w][0], 0.0)), parts)
            found[w] = x - dot3(parts, split(right))
        k *= 2
    found = [x * diagonals[w][1] for w, x in enumerate(found)]
    done = {}
    for w in range(count):
        done[w, w] = split(found[w])
        out_ref[0, w * window:(w + 1) * window, w * window:(w + 1) * window] = found[w]
    for gap in range(1, count):
        for c in range(count - gap):
            r = c + gap
            total = None
            for m in range(c, r):
                below = split(l_ref[0, 0, r * window:(r + 1) * window, m * window:(m + 1) * window])
                term = dot3(below, done[m, c])
                total = term if total is None else total + term
            value = -dot3(done[r, r], split(total))
            done[r, c] = split(value)
            out_ref[0, r * window:(r + 1) * window, c * window:(c + 1) * window] = value
            out_ref[0, c * window:(c + 1) * window, r * window:(r + 1) * window] = jnp.zeros(
                (window, window), F32
            )


def inverses(diag_factor):
    levels, size = diag_factor.shape[1], diag_factor.shape[-1]
    return pl.pallas_call(
        functools.partial(inverse_kernel, size, size // 3),
        grid=(levels,),
        in_specs=[pl.BlockSpec((1, 1, size, size), lambda i: (0, i, 0, 0))],
        out_specs=pl.BlockSpec((1, size, size), lambda i: (i, 0, 0)),
        out_shape=jax.ShapeDtypeStruct((levels, size, size), F32),
        compiler_params=pltpu.CompilerParams(vmem_limit_bytes=48 * 2**20),
        name="inverses",
    )(diag_factor)


def nt(a, b):
    return lax.dot_general(a, b, (((1,), (1,)), ((), ())), preferred_element_type=F32)


def nt3(a, b):
    return nt(a[0], b[0]) + (nt(a[1], b[0]) + nt(a[0], b[1]))


def inverse_steps(low, inv, level, starts):
    found, scaled, downs, pairs, eyes = [], [], [], [], []
    for at, to in starts:
        span = to - at
        row = lax.broadcasted_iota(jnp.int32, (span, span), 0)
        col = lax.broadcasted_iota(jnp.int32, (span, span), 1)
        eye = row == col
        block = low[level, at:to, at:to]
        down = 1.0 / jnp.sum(jnp.where(eye, block, 0.0), axis=1, keepdims=True)
        scaled.append(jnp.where(row > col, block * down, 0.0))
        downs.append(down)
        pairs.append(row ^ col)
        eyes.append(jnp.where(eye, 1.0, 0.0))
        first = split(jnp.where(pairs[-1] == 1, scaled[-1], 0.0))
        unit = eyes[-1].astype(BF)
        found.append(eyes[-1] - (nt(unit, first[0]) + nt(unit, first[1])))
    yield
    k = 2
    while k < starts[0][1] - starts[0][0]:
        for w, (at, to) in enumerate(starts):
            if k < to - at:
                parts = split(found[w])
                pair = (pairs[w] >= k) & (pairs[w] < 2 * k)
                right = nt3(parts, split(jnp.where(pair, scaled[w], 0.0)))
                found[w] = found[w] - dot3(split(right), parts)
        k *= 2
        yield
    done = {}

    def keep(c, r, value):
        done[c, r] = split(value)
        rows, columns = slice(*starts[c]), slice(*starts[r])
        inv[0, level, rows, columns] = done[c, r][0]
        inv[1, level, rows, columns] = done[c, r][1]

    for w in range(len(starts)):
        keep(w, w, found[w] * downs[w])
    for gap in range(1, len(starts)):
        for c in range(len(starts) - gap):
            r = c + gap
            total = None
            for m in range(c, r):
                below = split(low[level, slice(*starts[r]), slice(*starts[m])])
                term = nt3(done[c, m], below)
                total = term if total is None else total + term
            keep(c, r, -dot3(split(total), done[r, r]))
            zero = jnp.zeros((starts[r][1] - starts[r][0], starts[c][1] - starts[c][0]), BF)
            inv[0, level, slice(*starts[r]), slice(*starts[c])] = zero
            inv[1, level, slice(*starts[r]), slice(*starts[c])] = zero
        yield


def pack(x):
    rows, columns = x.shape
    full = columns // 128 * 128
    pieces = [x[:, at:at + 128] for at in range(0, full, 128)]
    rest = jnp.concatenate([x[:rows // 2, full:], x[rows // 2:, full:]], axis=1)
    return jnp.concatenate([*pieces, rest], axis=0)


def unpack(x, columns):
    rows = x.shape[0] * 128 // columns
    full = columns // 128
    pieces = [x[i * rows:(i + 1) * rows] for i in range(full)]
    rest = x[full * rows:]
    return jnp.concatenate(
        [*pieces, jnp.concatenate([rest[:, :64], rest[:, 64:]], axis=0)], axis=1
    )


def whole_kernel(size, parts, tiles, root_in, low_in, panel_in, chain_in, panel_out, block_out,
                 low, pf, ch, root, inv, sc, ct, pt, acc, gram, own_sum, sp, g1, g1s, g2, g2s, ar, ars,
                 load_s, pf_s, pf_r, root_s, root_r, fwd_s, fwd_r, sc_s, sc_r, pt_s, pt_r,
                 a_s, a_r, b_s, b_r, x_s, v_s, v_r, out_s, out_r):
    half = size // 2
    step = half // parts
    packed = step * size // 128
    branch = lax.axis_index("branch")
    me = lax.axis_index("row")
    z = me // 2
    core = me % 2
    side = z // 2
    outer, near, across, beyond = 3 * side, 1 + side, 2 - side, 3 - 3 * side
    is_inner = z == near
    is_outer = z == outer
    own = pl.ds(pl.multiple_of(core * half, 32), half)
    sibling = {"row": 2 * z + 1 - core}

    def chip(at):
        return {"row": 2 * at + core}

    def copy(src, dst, send_sem, recv_sem, target):
        return pltpu.make_async_remote_copy(
            src_ref=src, dst_ref=dst, send_sem=send_sem, recv_sem=recv_sem,
            device_id=target, device_id_type=MESH,
        )

    barrier = pltpu.get_barrier_semaphore()
    peers = [sibling] + [chip((z + k) % 4) for k in (1, 2, 3)]
    peers += [{"branch": (branch + k) % 4} for k in (1, 2, 3)]
    for peer in peers:
        pl.semaphore_signal(barrier, inc=1, device_id=peer, device_id_type=MESH)

    loads = {}
    for i in range(3):
        loads["low", i] = pltpu.make_async_copy(low_in.at[0, i], low.at[i], load_s.at[i])
        loads["pf", i] = pltpu.make_async_copy(
            panel_in.at[0, i], pf.at[i, own], load_s.at[3 + i]
        )
    loads["ch", 0] = pltpu.make_async_copy(chain_in.at[0], ch, load_s.at[6])
    loads["root", 0] = pltpu.make_async_copy(root_in, root.at[branch, own], load_s.at[7])
    for key in (("low", 0), ("pf", 0), ("root", 0), ("low", 1), ("low", 2), ("pf", 1), ("pf", 2),
                ("ch", 0)):
        loads[key].start()
    pl.semaphore_wait(barrier, 7)

    pf_to = [
        copy(panel_in.at[0, i], pf.at[i, own], pf_s.at[i], pf_r.at[i], sibling) for i in range(3)
    ]
    root_to = [
        copy(root_in, root.at[branch, own], root_s.at[k - 1], root_r.at[k - 1],
             {"branch": (branch + k) % 4})
        for k in (1, 2, 3)
    ]
    root_own = copy(root_in, root.at[branch, own], fwd_s.at[0], fwd_r.at[0], sibling)
    root_on = []
    for k in (1, 2, 3):
        block = root.at[(branch + 4 - k) % 4, own]
        root_on.append(copy(block, block, fwd_s.at[k], fwd_r.at[k], sibling))
    pf_to[0].start()
    for k in range(3):
        root_to[k].start()
    root_own.start()
    pf_to[1].start()
    pf_to[2].start()

    first, second, third = tiles[0, 0], tiles[0, 1], tiles[0, 2]

    def among(tile, count):
        hit = tile == first
        if count > 1:
            hit = hit | (tile == second)
        if count > 2:
            hit = hit | (tile == third)
        return jnp.where(hit, 1.0, 0.0)

    kept = [among(z, 3), among(z, 2), among(z, 1)]
    near_in, beyond_in = among(near, 3), among(beyond, 3)
    a_index = jnp.where(is_outer & (beyond_in < 0.5), across, beyond)
    b_index = jnp.where(is_outer & (near_in > 0.5), near, across)
    other_index = jnp.where(z == first, second, first)

    bounds = list(range(0, size, 256)) + [size]
    starts = list(zip(bounds[:-1], bounds[1:]))

    def rows(k):
        return slice(k * packed, (k + 1) * packed)

    def own_rows(k):
        return pl.ds(pl.multiple_of(core * half + k * step, 32), step)

    def cut(value, k):
        return value[k * step:(k + 1) * step]

    def whole_of(ref, *index):
        return jnp.concatenate(
            [unpack(ref[(*index, rows(k))].astype(F32), size) for k in range(parts)], axis=0
        )

    def both(ref, *index):
        return ref[(0, *index)], ref[(1, *index)]

    def keep(ref, index, value):
        hi, lo = split(value)
        ref[(0, *index)] = hi
        ref[(1, *index)] = lo

    a_far = [copy(sp.at[0, rows(k)], g1.at[1, rows(k)], a_s.at[0, k], a_r.at[1, k],
                  chip(across)) for k in range(parts)]
    a_near = [copy(sp.at[0, rows(k)], g1.at[0, rows(k)], a_s.at[1, k], a_r.at[0, k],
                   chip(near)) for k in range(parts)]
    b_far = [copy(sp.at[0, rows(k)], g1.at[2, rows(k)], b_s.at[2, k], a_r.at[2, k],
                  chip(across)) for k in range(parts)]
    out_a = [copy(g1s.at[0, rows(k)], g1.at[1, rows(k)], b_s.at[0, k], a_r.at[1, k],
                  chip(outer)) for k in range(parts)]
    out_b = [copy(g1s.at[1, rows(k)], g1.at[2, rows(k)], b_s.at[1, k], a_r.at[2, k],
                  chip(outer)) for k in range(parts)]
    x_near = [copy(sp.at[1, rows(k)], g2.at[0, rows(k)], x_s.at[0, k], b_r.at[0, k],
                   chip(near)) for k in range(parts)]
    x_far = [copy(g2s.at[0, rows(k)], g2.at[1, rows(k)], x_s.at[1, k], b_r.at[1, k],
                  chip(across)) for k in range(parts)]
    x_out = [copy(g2s.at[1, rows(k)], g2.at[1, rows(k)], x_s.at[2, k], b_r.at[1, k],
                  chip(outer)) for k in range(parts)]
    steps = [(m, k) for m in range(5) for k in range(parts)]
    u_near, u_far, u_out = {}, {}, {}
    for m, k in steps:
        u_near[m, k] = copy(ars.at[0, m, rows(k)], ar.at[0, m, rows(k)], v_s.at[0, m, k],
                            v_r.at[0, m, k], chip(near))
        u_far[m, k] = copy(ars.at[0, m, rows(k)], ar.at[1, m, rows(k)], v_s.at[0, m, k],
                           v_r.at[1, m, k], chip(across))
        u_out[m, k] = copy(ars.at[1, m, rows(k)], ar.at[1, m, rows(k)], v_s.at[1, m, k],
                           v_r.at[1, m, k], chip(outer))
    sc_to = [copy(sc.at[:, i, own], sc.at[:, i, own], sc_s.at[i], sc_r.at[i], sibling)
             if i else None for i in (0, 1, 2)]
    pt_to = [copy(pt.at[:, i, own], pt.at[:, i, own], pt_s.at[i], pt_r.at[i], sibling)
             for i in range(3)]

    def forward_root(k):
        root_to[k].wait_recv()
        root_on[k].start()

    def relay_one(k):
        @pl.when(is_inner)
        def _():
            a_far[k].wait_recv()
            b_far[k].wait_recv()
            theirs = g1[2, rows(k)].astype(F32)
            g1s[0, rows(k)] = (
                beyond_in * g1[1, rows(k)].astype(F32) + (1.0 - beyond_in) * theirs
            ).astype(BF)
            g1s[1, rows(k)] = (
                near_in * sp[0, rows(k)].astype(F32) + (1.0 - near_in) * theirs
            ).astype(BF)
            out_a[k].start()
            out_b[k].start()

    def near_two(k):
        @pl.when(is_inner)
        def _():
            x_near[k].wait_recv()
            mine = sp[1, rows(k)].astype(F32)
            g2s[0, rows(k)] = (g2[0, rows(k)].astype(F32) + mine).astype(BF)
            x_far[k].start()

    def far_two(k):
        @pl.when(is_inner)
        def _():
            x_out[k].wait_recv()
            mine = sp[1, rows(k)].astype(F32)
            g2s[1, rows(k)] = (g2[1, rows(k)].astype(F32) + mine).astype(BF)
            x_out[k].start()

    def send_sum(m, value):
        for k in range(parts):
            mine = pack(cut(value, k))
            own_sum[m, rows(k)] = mine
            ars[0, m, rows(k)] = mine.astype(BF)

        @pl.when(is_outer)
        def _():
            for k in range(parts):
                u_near[m, k].start()

    def near_sum(m, k):
        @pl.when(is_inner)
        def _():
            u_near[m, k].wait_recv()
            upto = ar[0, m, rows(k)].astype(F32) + own_sum[m, rows(k)]
            ars[0, m, rows(k)] = upto.astype(BF)
            u_far[m, k].start()

    def far_sum(m, k):
        @pl.when(is_inner)
        def _():
            u_out[m, k].wait_recv()
            rest = ar[1, m, rows(k)].astype(F32) + own_sum[m, rows(k)]
            ars[1, m, rows(k)] = rest.astype(BF)
            u_out[m, k].start()
            own_sum[m, rows(k)] = rest + ar[0, m, rows(k)].astype(F32)

    def settle(m):
        @pl.when(is_outer)
        def _():
            for k in range(parts):
                u_out[m, k].wait_recv()
                own_sum[m, rows(k)] = own_sum[m, rows(k)] + ar[1, m, rows(k)].astype(F32)

    order = []
    for i in range(len(steps) + 1):
        if i < len(steps):
            order.append((near_sum, *steps[i]))
        if i:
            order.append((far_sum, *steps[i - 1]))
    order.reverse()

    def relay(count):
        for _ in range(min(count, len(order))):
            todo, m, k = order.pop()
            todo(m, k)

    loads["low", 0].wait()
    for _ in inverse_steps(low, inv, 0, starts):
        pass

    def scale(i):
        loads["pf", i].wait()
        pf_to[i].wait_recv()
        value = nt3(both(inv, i, own), split(pf[i])) * kept[i]
        keep(sc, (i, own), value)
        if i < 2:
            for k in range(parts):
                sp[i, rows(k)] = pack(cut(value, k)).astype(BF)

    scale(0)

    @pl.when(is_outer)
    def _():
        for k in range(parts):
            a_far[k].start()
            a_near[k].start()

    @pl.when(is_inner)
    def _():
        for k in range(parts):
            b_far[k].start()

    loads["low", 1].wait()
    for _ in inverse_steps(low, inv, 1, starts):
        pass
    scale(1)

    @pl.when(is_outer)
    def _():
        for k in range(parts):
            x_near[k].start()

    sc_to[1].start()
    relay_one(0)
    loads["low", 2].wait()
    for turn, _ in enumerate(inverse_steps(low, inv, 2, starts)):
        if turn == 3:
            for k in range(3):
                forward_root(k)
        if turn == 6:
            relay_one(1)
    scale(2)
    sc_to[2].start()
    relay_one(2)
    loads["ch", 0].wait()
    keep(ct, (0,), nt3(both(inv, 1), split(ch[0])))
    near_two(0)
    keep(ct, (1,), nt3(both(inv, 2), split(ch[1])))
    loads["root", 0].wait()
    root_own.wait_recv()
    for k in range(3):
        root_on[k].wait_recv()
    acc[...] = nt(sc[0, 0, own], root[z])

    @pl.when(is_inner)
    def _():
        for k in range(parts):
            a_near[k].wait_recv()
        acc[...] += nt(whole_of(g1, 0).astype(BF), root[outer])

    @pl.when(is_outer)
    def _():
        for k in range(parts):
            out_a[k].wait_recv()
            out_b[k].wait_recv()

    acc[...] += nt(whole_of(g1, 1).astype(BF), root[a_index])
    acc[...] += nt(whole_of(g1, 2).astype(BF), root[b_index])
    first_panel = acc[...] * -kept[0]
    keep(pt, (0, own), first_panel)
    pt_to[0].start()
    sc_to[1].wait_recv()
    send_sum(0, nt3(both(pt, 0, own), both(sc, 1)))
    near_two(1)
    pt_to[0].wait_recv()
    send_sum(1, nt3(both(sc, 0, own), both(pt, 0)))
    near_two(2)
    far_two(0)
    gram[0] = nt3(both(inv, 0, own), both(inv, 0))
    far_two(1)
    gram[1] = nt3(both(inv, 1, own), both(inv, 1))
    far_two(2)

    @pl.when(is_outer)
    def _():
        for k in range(parts):
            x_out[k].wait_recv()
        acc[...] = whole_of(g2, 1)

    @pl.when(is_inner)
    def _():
        acc[...] = whole_of(g2, 0) + whole_of(g2, 1)

    value = nt(sc[0, 1, own], root[z]) + nt(acc[...].astype(BF), root[other_index])
    value = (value + dot3(both(ct, 0, own), both(pt, 0))) * -kept[1]
    keep(pt, (1, own), value)
    pt_to[1].start()
    relay(1)
    sc_to[2].wait_recv()
    acc[...] = nt3(both(pt, 1, own), both(sc, 2))
    relay(1)
    pt_to[1].wait_recv()
    send_sum(2, nt3(both(sc, 1, own), both(pt, 1)))
    send_sum(3, acc[...])
    relay(2)

    value = nt(sc[0, 2, own], root[z])
    value = (value + dot3(both(ct, 1, own), both(pt, 1))) * -kept[2]
    keep(pt, (2, own), value)
    pt_to[2].start()
    relay(2)
    pt_to[2].wait_recv()
    send_sum(4, nt3(both(sc, 2, own), both(pt, 2)))
    relay(2)
    gram[2] = nt3(both(inv, 2, own), both(inv, 2))
    relay(2)
    pick = jnp.where(
        lax.broadcasted_iota(jnp.int32, (half, size), 1)
        == lax.broadcasted_iota(jnp.int32, (half, size), 0) + core * half,
        1.0, 0.0,
    ).astype(BF)
    for i in range(3):
        panel_out[0, i] = nt(pick, pt[0, i]) + nt(pick, pt[1, i])
        if i:
            relay(2)

    def give(index, value, sem):
        block_out[0, index, own] = value
        block = block_out.at[0, index, own]
        return copy(block, block, out_s.at[sem], out_r.at[sem], sibling)

    gives = {}
    settle(1)
    gives[0] = give(0, gram[0] - whole_of(own_sum, 1), 0)
    gives[0].start()
    relay(2)
    settle(0)
    gives[3] = give(3, -(whole_of(own_sum, 0) + nt3(split(block_out[0, 0, own]), both(ct, 0))), 3)
    gives[3].start()
    relay(2)
    gives[3].wait_recv()
    gram[1] = gram[1] - dot3(both(ct, 0, own), split(block_out[0, 3]))
    relay(2)
    settle(2)
    value = gram[1] - whole_of(own_sum, 2)
    gives[1] = give(1, value, 1)
    gives[1].start()
    relay(2)
    acc[...] = nt3(split(value), both(ct, 1))
    relay(4)
    settle(3)
    gives[4] = give(4, -(whole_of(own_sum, 3) + acc[...]), 4)
    gives[4].start()
    relay(2)
    gives[4].wait_recv()
    gram[2] = gram[2] - dot3(both(ct, 1, own), split(block_out[0, 4]))
    relay(len(order))
    settle(4)
    for k in range(parts):
        at = own_rows(k)
        block_out[0, 2, at] = gram[2, k * step:(k + 1) * step] - unpack(own_sum[4, rows(k)], size)
        block = block_out.at[0, 2, at]
        gives[5 + k] = copy(block, block, out_s.at[5 + k], out_r.at[5 + k], sibling)
        gives[5 + k].start()
    for i in (0, 1):
        gives[i].wait_recv()
    for k in range(parts):
        gives[5 + k].wait_recv()

    for one in [*pf_to, *root_to, root_own, *root_on, sc_to[1], sc_to[2], *pt_to, *gives.values()]:
        one.wait_send()

    @pl.when(is_outer)
    def _():
        for one in [*a_far, *a_near, *x_near, *u_near.values()]:
            one.wait_send()

    @pl.when(is_inner)
    def _():
        for one in [*b_far, *out_a, *out_b, *x_far, *x_out, *u_far.values(), *u_out.values()]:
            one.wait_send()


def whole(root_cov, diag_factor, panel_factor, chain_factor, panel_tiles):
    size = diag_factor.shape[-1]
    half = size // 2
    parts = 3
    line = half * size // 128
    dma = pltpu.SemaphoreType.DMA
    anywhere = pl.BlockSpec(memory_space=pl.ANY)
    inside = pl.BlockSpec(memory_space=pltpu.VMEM)
    vm = pltpu.VMEM
    return pl.pallas_call(
        functools.partial(whole_kernel, size, parts),
        out_shape=(vm((1, 3, half, size), F32), vm((1, 5, size, size), F32)),
        in_specs=[pl.BlockSpec(memory_space=pltpu.SMEM)] + [anywhere] * 4,
        out_specs=(inside, inside),
        scratch_shapes=[
            vm((3, size, size), F32),
            vm((3, size, size), F32),
            vm((2, size, size), F32),
            vm((4, size, size), BF),
            vm((2, 3, size, size), BF),
            vm((2, 3, size, size), BF),
            vm((2, 2, size, size), BF),
            vm((2, 3, size, size), BF),
            vm((half, size), F32),
            vm((3, half, size), F32),
            vm((5, line, 128), F32),
            vm((2, line, 128), BF),
            vm((3, line, 128), BF),
            vm((2, line, 128), BF),
            vm((2, line, 128), BF),
            vm((2, line, 128), BF),
            vm((2, 5, line, 128), BF),
            vm((2, 5, line, 128), BF),
            dma((8,)), dma((3,)), dma((3,)), dma((3,)), dma((3,)), dma((4,)), dma((4,)),
            dma((3,)), dma((3,)), dma((3,)), dma((3,)),
            dma((2, parts)), dma((3, parts)), dma((3, parts)), dma((2, parts)),
            dma((3, parts)), dma((2, 5, parts)), dma((2, 5, parts)), dma((5 + parts,)),
            dma((5 + parts,)),
        ],
        compiler_params=pltpu.CompilerParams(
            collective_id=0, has_side_effects=True, vmem_limit_bytes=52 * 2**20
        ),
        name="whole",
    )(panel_tiles, root_cov, diag_factor, panel_factor, chain_factor)


def on_device(root_cov, diag_factor, panel_factor, chain_factor, panel_tiles):
    node_width = diag_factor.shape[-1]
    rows_here = panel_factor.shape[2]
    per_tile = node_width // rows_here
    row_count = lax.axis_size("row")
    tile_total = row_count // per_tile
    counts = (3 * tile_total // 4, tile_total // 2, tile_total // 4)
    small = row_count == 8 and tile_total == 4 and root_cov.shape[1] == node_width
    if small:
        return whole(root_cov, diag_factor, panel_factor, chain_factor, panel_tiles)
    root_rows = lax.all_gather(root_cov, "branch", axis=1, tiled=True)
    me = lax.axis_index("row")
    my_tile = me // per_tile
    inverse_all = inverses(diag_factor)
    share = -(-node_width // row_count // 8) * 8
    padded = jnp.pad(inverse_all, ((0, 0), (0, share * row_count - node_width), (0, 0)))
    mine = lax.dynamic_slice_in_dim(padded, me * share, share, axis=1)
    chosen = [jnp.any(panel_tiles[0, : counts[i]] == my_tile) for i in range(3)]
    scaled = [
        jnp.where(chosen[i], product(panel_factor[0, i], inverse_all[i]), 0.0) for i in range(3)
    ]
    panels = []
    blocks = []
    crosses = []
    for i in range(3):
        rounded = scaled[i].astype(BF)
        gathered = jnp.dot(
            root_rows,
            lax.all_gather(rounded, "row", axis=0, tiled=True),
            preferred_element_type=F32,
        )
        left = jnp.concatenate([mine[i], scaled[i]], axis=0)
        if i == 0:
            panel = -jnp.where(chosen[i], gathered, 0.0)
            block = product(left.T, jnp.concatenate([mine[i], -panel], axis=0))
        else:
            chain = product(chain_factor[0, i - 1], inverse_all[i])
            panel = -jnp.where(chosen[i], gathered + product(panels[-1], chain), 0.0)
            cross = -(product(panels[-1].T, scaled[i]) + product(blocks[-1], chain))
            block = product(left.T, jnp.concatenate([mine[i], -panel], axis=0)) - product(
                chain.T, cross
            )
            crosses.append(cross)
        panels.append(panel)
        blocks.append(block)
    total = lax.psum(jnp.stack(blocks + crosses), "row")
    return (jnp.stack(panels)[None], total[None])


def solution(mesh):
    in_specs = (
        P("row", "branch"),
        P("branch", None, None, None),
        P("branch", None, "row", None),
        P("branch", None, None, None),
        P("branch", None),
    )
    out_specs = (P("branch", None, "row", None), P("branch", None, None, None))
    return jax.shard_map(
        on_device, mesh=mesh, in_specs=in_specs, out_specs=out_specs, check_vma=False
    )
```

```python
import functools
import jax
import jax.numpy as jnp
from jax import lax
from jax.experimental import pallas as pl
from jax.experimental.pallas import tpu as pltpu
from jax.sharding import PartitionSpec as P

BF = jnp.bfloat16
F32 = jnp.float32
MESH = pl.DeviceIdType.MESH


def product(left_mat, right_mat):
    return jnp.dot(left_mat, right_mat, precision=lax.Precision.HIGH, preferred_element_type=F32)


def split(x):
    hi = x.astype(BF)
    return hi, (x - hi.astype(F32)).astype(BF)


def mm(a, b):
    return jnp.dot(a, b, preferred_element_type=F32)


def dot3(a, b):
    a_hi, a_lo = a
    b_hi, b_lo = b
    return mm(a_hi, b_hi) + (mm(a_lo, b_hi) + mm(a_hi, b_lo))


def inverse_kernel(size, window, l_ref, out_ref):
    count = size // window
    row = lax.broadcasted_iota(jnp.int32, (window, window), 0)
    col = lax.broadcasted_iota(jnp.int32, (window, window), 1)
    eye = row == col
    diagonals = []
    for w in range(count):
        at = slice(w * window, (w + 1) * window)
        block = l_ref[0, 0, at, at]
        kept = jnp.where(eye, block, 0.0)
        down = 1.0 / jnp.sum(kept, axis=1, keepdims=True)
        across = 1.0 / jnp.sum(kept, axis=0, keepdims=True)
        diagonals.append((block * down, across))
    found = []
    for scaled, across in diagonals:
        x = jnp.where(eye, 1.0, 0.0)
        x = x - jnp.where((row // 2 == col // 2) & (row > col), scaled, 0.0)
        found.append(x)
    k = 2
    while k < window:
        pair = (row // (2 * k) == col // (2 * k)) & (row // k > col // k)
        for w in range(count):
            x = found[w]
            parts = split(x)
            right = dot3(split(jnp.where(pair, diagonals[w][0], 0.0)), parts)
            found[w] = x - dot3(parts, split(right))
        k *= 2
    found = [x * diagonals[w][1] for w, x in enumerate(found)]
    done = {}
    for w in range(count):
        done[w, w] = split(found[w])
        out_ref[0, w * window:(w + 1) * window, w * window:(w + 1) * window] = found[w]
    for gap in range(1, count):
        for c in range(count - gap):
            r = c + gap
            total = None
            for m in range(c, r):
                below = split(l_ref[0, 0, r * window:(r + 1) * window, m * window:(m + 1) * window])
                term = dot3(below, done[m, c])
                total = term if total is None else total + term
            value = -dot3(done[r, r], split(total))
            done[r, c] = split(value)
            out_ref[0, r * window:(r + 1) * window, c * window:(c + 1) * window] = value
            out_ref[0, c * window:(c + 1) * window, r * window:(r + 1) * window] = jnp.zeros(
                (window, window), F32
            )


def inverses(diag_factor):
    levels, size = diag_factor.shape[1], diag_factor.shape[-1]
    return pl.pallas_call(
        functools.partial(inverse_kernel, size, size // 3),
        grid=(levels,),
        in_specs=[pl.BlockSpec((1, 1, size, size), lambda i: (0, i, 0, 0))],
        out_specs=pl.BlockSpec((1, size, size), lambda i: (i, 0, 0)),
        out_shape=jax.ShapeDtypeStruct((levels, size, size), F32),
        compiler_params=pltpu.CompilerParams(vmem_limit_bytes=48 * 2**20),
        name="inverses",
    )(diag_factor)


def nt(a, b):
    return lax.dot_general(a, b, (((1,), (1,)), ((), ())), preferred_element_type=F32)


def nt3(a, b):
    return nt(a[0], b[0]) + (nt(a[1], b[0]) + nt(a[0], b[1]))


def nt2(a, b):
    return nt(a, b[0]) + nt(a, b[1])


def inverse_steps(low, inv, level, starts):
    found, scaled, downs, pairs, eyes = [], [], [], [], []
    for at, to in starts:
        span = to - at
        row = lax.broadcasted_iota(jnp.int32, (span, span), 0)
        col = lax.broadcasted_iota(jnp.int32, (span, span), 1)
        eye = row == col
        block = low[level, at:to, at:to]
        down = 1.0 / jnp.sum(jnp.where(eye, block, 0.0), axis=1, keepdims=True)
        scaled.append(jnp.where(row > col, block * down, 0.0))
        downs.append(down)
        pairs.append(row ^ col)
        eyes.append(jnp.where(eye, 1.0, 0.0))
        first = split(jnp.where(pairs[-1] == 1, scaled[-1], 0.0))
        unit = eyes[-1].astype(BF)
        found.append(eyes[-1] - (nt(unit, first[0]) + nt(unit, first[1])))
    yield
    k = 2
    while k < starts[0][1] - starts[0][0]:
        for w, (at, to) in enumerate(starts):
            if k < to - at:
                parts = split(found[w])
                pair = (pairs[w] >= k) & (pairs[w] < 2 * k)
                right = nt3(parts, split(jnp.where(pair, scaled[w], 0.0)))
                found[w] = found[w] - dot3(split(right), parts)
        k *= 2
        yield
    done = {}

    def keep(c, r, value):
        done[c, r] = split(value)
        rows, columns = slice(*starts[c]), slice(*starts[r])
        inv[0, level, rows, columns] = done[c, r][0]
        inv[1, level, rows, columns] = done[c, r][1]

    for w in range(len(starts)):
        keep(w, w, found[w] * downs[w])
    for gap in range(1, len(starts)):
        for c in range(len(starts) - gap):
            r = c + gap
            total = None
            for m in range(c, r):
                below = split(low[level, slice(*starts[r]), slice(*starts[m])])
                term = nt3(done[c, m], below)
                total = term if total is None else total + term
            keep(c, r, -dot3(split(total), done[r, r]))
            zero = jnp.zeros((starts[r][1] - starts[r][0], starts[c][1] - starts[c][0]), BF)
            inv[0, level, slice(*starts[r]), slice(*starts[c])] = zero
            inv[1, level, slice(*starts[r]), slice(*starts[c])] = zero
        yield


def pack(x):
    rows, columns = x.shape
    full = columns // 128 * 128
    pieces = [x[:, at:at + 128] for at in range(0, full, 128)]
    rest = jnp.concatenate([x[:rows // 2, full:], x[rows // 2:, full:]], axis=1)
    return jnp.concatenate([*pieces, rest], axis=0)


def unpack(x, columns):
    rows = x.shape[0] * 128 // columns
    full = columns // 128
    pieces = [x[i * rows:(i + 1) * rows] for i in range(full)]
    rest = x[full * rows:]
    return jnp.concatenate(
        [*pieces, jnp.concatenate([rest[:, :64], rest[:, 64:]], axis=0)], axis=1
    )


def whole_kernel(size, parts, tiles, root_in, low_in, panel_in, chain_in, panel_out, block_out,
                 low, pf, ch, root, inv, sc, ct, pt, acc, gram, own_sum, sp, g1, g1s, g2, g2s, ar, ars,
                 load_s, pf_s, pf_r, root_s, root_r, fwd_s, fwd_r, sc_s, sc_r, pt_s, pt_r,
                 a_s, a_r, b_s, b_r, x_s, v_s, v_r, out_s, out_r):
    half = size // 2
    step = half // parts
    packed = step * size // 128
    branch = lax.axis_index("branch")
    me = lax.axis_index("row")
    z = me // 2
    core = me % 2
    side = z // 2
    outer, near, across, beyond = 3 * side, 1 + side, 2 - side, 3 - 3 * side
    is_inner = z == near
    is_outer = z == outer
    own = pl.ds(pl.multiple_of(core * half, 32), half)
    sibling = {"row": 2 * z + 1 - core}

    def chip(at):
        return {"row": 2 * at + core}

    def copy(src, dst, send_sem, recv_sem, target):
        return pltpu.make_async_remote_copy(
            src_ref=src, dst_ref=dst, send_sem=send_sem, recv_sem=recv_sem,
            device_id=target, device_id_type=MESH,
        )

    barrier = pltpu.get_barrier_semaphore()
    peers = [sibling] + [chip((z + k) % 4) for k in (1, 2, 3)]
    peers += [{"branch": (branch + k) % 4} for k in (1, 2, 3)]
    for peer in peers:
        pl.semaphore_signal(barrier, inc=1, device_id=peer, device_id_type=MESH)

    loads = {}
    for i in range(3):
        loads["low", i] = pltpu.make_async_copy(low_in.at[0, i], low.at[i], load_s.at[i])
        loads["pf", i] = pltpu.make_async_copy(
            panel_in.at[0, i], pf.at[i, own], load_s.at[3 + i]
        )
    loads["ch", 0] = pltpu.make_async_copy(chain_in.at[0], ch, load_s.at[6])
    loads["root", 0] = pltpu.make_async_copy(root_in, root.at[branch, own], load_s.at[7])
    for key in (("low", 0), ("pf", 0), ("root", 0), ("low", 1), ("low", 2), ("pf", 1), ("pf", 2),
                ("ch", 0)):
        loads[key].start()
    pl.semaphore_wait(barrier, 7)

    pf_to = [
        copy(panel_in.at[0, i], pf.at[i, own], pf_s.at[i], pf_r.at[i], sibling) for i in range(3)
    ]
    root_to = [
        copy(root_in, root.at[branch, own], root_s.at[k - 1], root_r.at[k - 1],
             {"branch": (branch + k) % 4})
        for k in (1, 2, 3)
    ]
    root_own = copy(root_in, root.at[branch, own], fwd_s.at[0], fwd_r.at[0], sibling)
    root_on = []
    for k in (1, 2, 3):
        block = root.at[(branch + 4 - k) % 4, own]
        root_on.append(copy(block, block, fwd_s.at[k], fwd_r.at[k], sibling))
    pf_to[0].start()
    for k in range(3):
        root_to[k].start()
    root_own.start()
    pf_to[1].start()
    pf_to[2].start()

    first, second, third = tiles[0, 0], tiles[0, 1], tiles[0, 2]

    def among(tile, count):
        hit = tile == first
        if count > 1:
            hit = hit | (tile == second)
        if count > 2:
            hit = hit | (tile == third)
        return jnp.where(hit, 1.0, 0.0)

    kept = [among(z, 3), among(z, 2), among(z, 1)]
    near_in, beyond_in = among(near, 3), among(beyond, 3)
    a_index = jnp.where(is_outer & (beyond_in < 0.5), across, beyond)
    b_index = jnp.where(is_outer & (near_in > 0.5), near, across)
    other_index = jnp.where(z == first, second, first)

    bounds = list(range(0, size, 256)) + [size]
    starts = list(zip(bounds[:-1], bounds[1:]))

    def rows(k):
        return slice(k * packed, (k + 1) * packed)

    def own_rows(k):
        return pl.ds(pl.multiple_of(core * half + k * step, 32), step)

    def cut(value, k):
        return value[k * step:(k + 1) * step]

    def whole_of(ref, *index):
        return jnp.concatenate(
            [unpack(ref[(*index, rows(k))].astype(F32), size) for k in range(parts)], axis=0
        )

    def both(ref, *index):
        return ref[(0, *index)], ref[(1, *index)]

    def keep(ref, index, value):
        hi, lo = split(value)
        ref[(0, *index)] = hi
        ref[(1, *index)] = lo

    a_far = [copy(sp.at[0, rows(k)], g1.at[1, rows(k)], a_s.at[0, k], a_r.at[1, k],
                  chip(across)) for k in range(parts)]
    a_near = [copy(sp.at[0, rows(k)], g1.at[0, rows(k)], a_s.at[1, k], a_r.at[0, k],
                   chip(near)) for k in range(parts)]
    b_far = [copy(sp.at[0, rows(k)], g1.at[2, rows(k)], b_s.at[2, k], a_r.at[2, k],
                  chip(across)) for k in range(parts)]
    out_a = [copy(g1s.at[0, rows(k)], g1.at[1, rows(k)], b_s.at[0, k], a_r.at[1, k],
                  chip(outer)) for k in range(parts)]
    out_b = [copy(g1s.at[1, rows(k)], g1.at[2, rows(k)], b_s.at[1, k], a_r.at[2, k],
                  chip(outer)) for k in range(parts)]
    x_near = [copy(sp.at[1, rows(k)], g2.at[0, rows(k)], x_s.at[0, k], b_r.at[0, k],
                   chip(near)) for k in range(parts)]
    x_far = [copy(g2s.at[0, rows(k)], g2.at[1, rows(k)], x_s.at[1, k], b_r.at[1, k],
                  chip(across)) for k in range(parts)]
    x_out = [copy(g2s.at[1, rows(k)], g2.at[1, rows(k)], x_s.at[2, k], b_r.at[1, k],
                  chip(outer)) for k in range(parts)]
    steps = [(m, k) for m in range(5) for k in range(parts)]
    u_near, u_far, u_out = {}, {}, {}
    for m, k in steps:
        u_near[m, k] = copy(ars.at[0, m, rows(k)], ar.at[0, m, rows(k)], v_s.at[0, m, k],
                            v_r.at[0, m, k], chip(near))
        u_far[m, k] = copy(ars.at[0, m, rows(k)], ar.at[1, m, rows(k)], v_s.at[0, m, k],
                           v_r.at[1, m, k], chip(across))
        u_out[m, k] = copy(ars.at[1, m, rows(k)], ar.at[1, m, rows(k)], v_s.at[1, m, k],
                           v_r.at[1, m, k], chip(outer))
    sc_to = [copy(sc.at[0, i, own], sc.at[0, i, own], sc_s.at[i], sc_r.at[i], sibling)
             if i else None for i in (0, 1, 2)]
    pt_to = [copy(pt.at[:, i, own], pt.at[:, i, own], pt_s.at[i], pt_r.at[i], sibling)
             for i in range(3)]

    def forward_root(k):
        root_to[k].wait_recv()
        root_on[k].start()

    def relay_one(k):
        @pl.when(is_inner)
        def _():
            a_far[k].wait_recv()
            b_far[k].wait_recv()
            theirs = g1[2, rows(k)].astype(F32)
            g1s[0, rows(k)] = (
                beyond_in * g1[1, rows(k)].astype(F32) + (1.0 - beyond_in) * theirs
            ).astype(BF)
            g1s[1, rows(k)] = (
                near_in * sp[0, rows(k)].astype(F32) + (1.0 - near_in) * theirs
            ).astype(BF)
            out_a[k].start()
            out_b[k].start()

    def near_two(k):
        @pl.when(is_inner)
        def _():
            x_near[k].wait_recv()
            mine = sp[1, rows(k)].astype(F32)
            g2s[0, rows(k)] = (g2[0, rows(k)].astype(F32) + mine).astype(BF)
            x_far[k].start()

    def far_two(k):
        @pl.when(is_inner)
        def _():
            x_out[k].wait_recv()
            mine = sp[1, rows(k)].astype(F32)
            g2s[1, rows(k)] = (g2[1, rows(k)].astype(F32) + mine).astype(BF)
            x_out[k].start()

    def send_sum(m, value):
        for k in range(parts):
            mine = pack(cut(value, k))
            own_sum[m, rows(k)] = mine
            ars[0, m, rows(k)] = mine.astype(BF)

        @pl.when(is_outer)
        def _():
            for k in range(parts):
                u_near[m, k].start()

    def near_sum(m, k):
        @pl.when(is_inner)
        def _():
            u_near[m, k].wait_recv()
            upto = ar[0, m, rows(k)].astype(F32) + own_sum[m, rows(k)]
            ars[0, m, rows(k)] = upto.astype(BF)
            u_far[m, k].start()

    def far_sum(m, k):
        @pl.when(is_inner)
        def _():
            u_out[m, k].wait_recv()
            rest = ar[1, m, rows(k)].astype(F32) + own_sum[m, rows(k)]
            ars[1, m, rows(k)] = rest.astype(BF)
            u_out[m, k].start()
            own_sum[m, rows(k)] = rest + ar[0, m, rows(k)].astype(F32)

    def settle(m):
        @pl.when(is_outer)
        def _():
            for k in range(parts):
                u_out[m, k].wait_recv()
                own_sum[m, rows(k)] = own_sum[m, rows(k)] + ar[1, m, rows(k)].astype(F32)

    order = []
    for i in range(len(steps) + 1):
        if i < len(steps):
            order.append((near_sum, *steps[i]))
        if i:
            order.append((far_sum, *steps[i - 1]))
    order.reverse()

    def relay(count):
        for _ in range(min(count, len(order))):
            todo, m, k = order.pop()
            todo(m, k)

    loads["low", 0].wait()
    for _ in inverse_steps(low, inv, 0, starts):
        pass

    def gram_of(i):
        return jnp.concatenate(
            [nt3(both(inv, i, own, slice(at, size)), both(inv, i, slice(at, to), slice(at, size)))
             for at, to in starts], axis=1,
        )

    def chain_of(i):
        hi, lo = split(ch[i])
        for at, to in starts:
            part = nt3(both(inv, i + 1, slice(at, to), slice(at, size)), (hi[:, at:], lo[:, at:]))
            keep(ct, (i, slice(at, to)), part)

    def scale(i):
        loads["pf", i].wait()
        pf_to[i].wait_recv()
        value = nt3(both(inv, i, own), split(pf[i])) * kept[i]
        keep(sc, (i, own), value)
        if i < 2:
            for k in range(parts):
                sp[i, rows(k)] = pack(cut(value, k)).astype(BF)

    scale(0)

    @pl.when(is_outer)
    def _():
        for k in range(parts):
            a_far[k].start()
            a_near[k].start()

    @pl.when(is_inner)
    def _():
        for k in range(parts):
            b_far[k].start()

    loads["low", 1].wait()
    for _ in inverse_steps(low, inv, 1, starts):
        pass
    scale(1)

    @pl.when(is_outer)
    def _():
        for k in range(parts):
            x_near[k].start()

    sc_to[1].start()
    relay_one(0)
    loads["low", 2].wait()
    for turn, _ in enumerate(inverse_steps(low, inv, 2, starts)):
        if turn == 3:
            for k in range(3):
                forward_root(k)
        if turn == 6:
            relay_one(1)
    scale(2)
    sc_to[2].start()
    relay_one(2)
    loads["ch", 0].wait()
    chain_of(0)
    near_two(0)
    chain_of(1)
    loads["root", 0].wait()
    root_own.wait_recv()
    for k in range(3):
        root_on[k].wait_recv()
    acc[...] = nt(sc[0, 0, own], root[z])

    @pl.when(is_inner)
    def _():
        for k in range(parts):
            a_near[k].wait_recv()
        acc[...] += nt(whole_of(g1, 0).astype(BF), root[outer])

    @pl.when(is_outer)
    def _():
        for k in range(parts):
            out_a[k].wait_recv()
            out_b[k].wait_recv()

    acc[...] += nt(whole_of(g1, 1).astype(BF), root[a_index])
    acc[...] += nt(whole_of(g1, 2).astype(BF), root[b_index])
    first_panel = acc[...] * -kept[0]
    keep(pt, (0, own), first_panel)
    pt_to[0].start()
    sc_to[1].wait_recv()
    send_sum(0, nt(pt[0, 0, own], sc[0, 1]) + nt(pt[1, 0, own], sc[0, 1]))
    near_two(1)
    pt_to[0].wait_recv()
    send_sum(1, nt2(sc[0, 0, own], both(pt, 0)))
    near_two(2)
    far_two(0)
    gram[0] = gram_of(0)
    far_two(1)
    gram[1] = gram_of(1)
    far_two(2)

    @pl.when(is_outer)
    def _():
        for k in range(parts):
            x_out[k].wait_recv()
        acc[...] = whole_of(g2, 1)

    @pl.when(is_inner)
    def _():
        acc[...] = whole_of(g2, 0) + whole_of(g2, 1)

    value = nt(sc[0, 1, own], root[z]) + nt(acc[...].astype(BF), root[other_index])
    value = (value + dot3(both(ct, 0, own), both(pt, 0))) * -kept[1]
    keep(pt, (1, own), value)
    pt_to[1].start()
    relay(1)
    sc_to[2].wait_recv()
    acc[...] = nt(pt[0, 1, own], sc[0, 2]) + nt(pt[1, 1, own], sc[0, 2])
    relay(1)
    pt_to[1].wait_recv()
    send_sum(2, nt2(sc[0, 1, own], both(pt, 1)))
    send_sum(3, acc[...])
    relay(2)

    value = nt(sc[0, 2, own], root[z])
    value = (value + dot3(both(ct, 1, own), both(pt, 1))) * -kept[2]
    keep(pt, (2, own), value)
    pt_to[2].start()
    relay(2)
    pt_to[2].wait_recv()
    send_sum(4, nt2(sc[0, 2, own], both(pt, 2)))
    relay(2)
    gram[2] = gram_of(2)
    relay(2)
    pick = jnp.where(
        lax.broadcasted_iota(jnp.int32, (half, size), 1)
        == lax.broadcasted_iota(jnp.int32, (half, size), 0) + core * half,
        1.0, 0.0,
    ).astype(BF)
    for i in range(3):
        panel_out[0, i] = nt(pick, pt[0, i]) + nt(pick, pt[1, i])
        if i:
            relay(2)

    def give(index, value, sem):
        block_out[0, index, own] = value
        block = block_out.at[0, index, own]
        return copy(block, block, out_s.at[sem], out_r.at[sem], sibling)

    gives = {}
    settle(1)
    gives[0] = give(0, gram[0] - whole_of(own_sum, 1), 0)
    gives[0].start()
    relay(2)
    settle(0)
    gives[3] = give(3, -(whole_of(own_sum, 0) + nt3(split(block_out[0, 0, own]), both(ct, 0))), 3)
    gives[3].start()
    relay(2)
    gives[3].wait_recv()
    gram[1] = gram[1] - dot3(both(ct, 0, own), split(block_out[0, 3]))
    relay(2)
    settle(2)
    value = gram[1] - whole_of(own_sum, 2)
    gives[1] = give(1, value, 1)
    gives[1].start()
    relay(2)
    acc[...] = nt3(split(value), both(ct, 1))
    relay(4)
    settle(3)
    gives[4] = give(4, -(whole_of(own_sum, 3) + acc[...]), 4)
    gives[4].start()
    relay(2)
    gives[4].wait_recv()
    gram[2] = gram[2] - dot3(both(ct, 1, own), split(block_out[0, 4]))
    relay(len(order))
    settle(4)
    for k in range(parts):
        at = own_rows(k)
        block_out[0, 2, at] = gram[2, k * step:(k + 1) * step] - unpack(own_sum[4, rows(k)], size)
        block = block_out.at[0, 2, at]
        gives[5 + k] = copy(block, block, out_s.at[5 + k], out_r.at[5 + k], sibling)
        gives[5 + k].start()
    for i in (0, 1):
        gives[i].wait_recv()
    for k in range(parts):
        gives[5 + k].wait_recv()

    for one in [*pf_to, *root_to, root_own, *root_on, sc_to[1], sc_to[2], *pt_to, *gives.values()]:
        one.wait_send()

    @pl.when(is_outer)
    def _():
        for one in [*a_far, *a_near, *x_near, *u_near.values()]:
            one.wait_send()

    @pl.when(is_inner)
    def _():
        for one in [*b_far, *out_a, *out_b, *x_far, *x_out, *u_far.values(), *u_out.values()]:
            one.wait_send()


def whole(root_cov, diag_factor, panel_factor, chain_factor, panel_tiles):
    size = diag_factor.shape[-1]
    half = size // 2
    parts = 3
    line = half * size // 128
    dma = pltpu.SemaphoreType.DMA
    anywhere = pl.BlockSpec(memory_space=pl.ANY)
    inside = pl.BlockSpec(memory_space=pltpu.VMEM)
    vm = pltpu.VMEM
    return pl.pallas_call(
        functools.partial(whole_kernel, size, parts),
        out_shape=(vm((1, 3, half, size), F32), vm((1, 5, size, size), F32)),
        in_specs=[pl.BlockSpec(memory_space=pltpu.SMEM)] + [anywhere] * 4,
        out_specs=(inside, inside),
        scratch_shapes=[
            vm((3, size, size), F32),
            vm((3, size, size), F32),
            vm((2, size, size), F32),
            vm((4, size, size), BF),
            vm((2, 3, size, size), BF),
            vm((2, 3, size, size), BF),
            vm((2, 2, size, size), BF),
            vm((2, 3, size, size), BF),
            vm((half, size), F32),
            vm((3, half, size), F32),
            vm((5, line, 128), F32),
            vm((2, line, 128), BF),
            vm((3, line, 128), BF),
            vm((2, line, 128), BF),
            vm((2, line, 128), BF),
            vm((2, line, 128), BF),
            vm((2, 5, line, 128), BF),
            vm((2, 5, line, 128), BF),
            dma((8,)), dma((3,)), dma((3,)), dma((3,)), dma((3,)), dma((4,)), dma((4,)),
            dma((3,)), dma((3,)), dma((3,)), dma((3,)),
            dma((2, parts)), dma((3, parts)), dma((3, parts)), dma((2, parts)),
            dma((3, parts)), dma((2, 5, parts)), dma((2, 5, parts)), dma((5 + parts,)),
            dma((5 + parts,)),
        ],
        compiler_params=pltpu.CompilerParams(
            collective_id=0, has_side_effects=True, vmem_limit_bytes=52 * 2**20
        ),
        name="whole",
    )(panel_tiles, root_cov, diag_factor, panel_factor, chain_factor)


def on_device(root_cov, diag_factor, panel_factor, chain_factor, panel_tiles):
    node_width = diag_factor.shape[-1]
    rows_here = panel_factor.shape[2]
    per_tile = node_width // rows_here
    row_count = lax.axis_size("row")
    tile_total = row_count // per_tile
    counts = (3 * tile_total // 4, tile_total // 2, tile_total // 4)
    small = row_count == 8 and tile_total == 4 and root_cov.shape[1] == node_width
    if small:
        return whole(root_cov, diag_factor, panel_factor, chain_factor, panel_tiles)
    root_rows = lax.all_gather(root_cov, "branch", axis=1, tiled=True)
    me = lax.axis_index("row")
    my_tile = me // per_tile
    inverse_all = inverses(diag_factor)
    share = -(-node_width // row_count // 8) * 8
    padded = jnp.pad(inverse_all, ((0, 0), (0, share * row_count - node_width), (0, 0)))
    mine = lax.dynamic_slice_in_dim(padded, me * share, share, axis=1)
    chosen = [jnp.any(panel_tiles[0, : counts[i]] == my_tile) for i in range(3)]
    scaled = [
        jnp.where(chosen[i], product(panel_factor[0, i], inverse_all[i]), 0.0) for i in range(3)
    ]
    panels = []
    blocks = []
    crosses = []
    for i in range(3):
        rounded = scaled[i].astype(BF)
        gathered = jnp.dot(
            root_rows,
            lax.all_gather(rounded, "row", axis=0, tiled=True),
            preferred_element_type=F32,
        )
        left = jnp.concatenate([mine[i], scaled[i]], axis=0)
        if i == 0:
            panel = -jnp.where(chosen[i], gathered, 0.0)
            block = product(left.T, jnp.concatenate([mine[i], -panel], axis=0))
        else:
            chain = product(chain_factor[0, i - 1], inverse_all[i])
            panel = -jnp.where(chosen[i], gathered + product(panels[-1], chain), 0.0)
            cross = -(product(panels[-1].T, scaled[i]) + product(blocks[-1], chain))
            block = product(left.T, jnp.concatenate([mine[i], -panel], axis=0)) - product(
                chain.T, cross
            )
            crosses.append(cross)
        panels.append(panel)
        blocks.append(block)
    total = lax.psum(jnp.stack(blocks + crosses), "row")
    return (jnp.stack(panels)[None], total[None])


def solution(mesh):
    in_specs = (
        P("row", "branch"),
        P("branch", None, None, None),
        P("branch", None, "row", None),
        P("branch", None, None, None),
        P("branch", None),
    )
    out_specs = (P("branch", None, "row", None), P("branch", None, None, None))
    return jax.shard_map(
        on_device, mesh=mesh, in_specs=in_specs, out_specs=out_specs, check_vma=False
    )
```

```python
import functools
import jax
import jax.numpy as jnp
from jax import lax
from jax.experimental import pallas as pl
from jax.experimental.pallas import tpu as pltpu
from jax.sharding import PartitionSpec as P

BF = jnp.bfloat16
F32 = jnp.float32
MESH = pl.DeviceIdType.MESH


def product(left_mat, right_mat):
    return jnp.dot(left_mat, right_mat, precision=lax.Precision.HIGH, preferred_element_type=F32)


def split(x):
    hi = x.astype(BF)
    return hi, (x - hi.astype(F32)).astype(BF)


def mm(a, b):
    return jnp.dot(a, b, preferred_element_type=F32)


def dot3(a, b):
    a_hi, a_lo = a
    b_hi, b_lo = b
    return mm(a_hi, b_hi) + (mm(a_lo, b_hi) + mm(a_hi, b_lo))


def inverse_kernel(size, window, l_ref, out_ref):
    count = size // window
    row = lax.broadcasted_iota(jnp.int32, (window, window), 0)
    col = lax.broadcasted_iota(jnp.int32, (window, window), 1)
    eye = row == col
    diagonals = []
    for w in range(count):
        at = slice(w * window, (w + 1) * window)
        block = l_ref[0, 0, at, at]
        kept = jnp.where(eye, block, 0.0)
        down = 1.0 / jnp.sum(kept, axis=1, keepdims=True)
        across = 1.0 / jnp.sum(kept, axis=0, keepdims=True)
        diagonals.append((block * down, across))
    found = []
    for scaled, across in diagonals:
        x = jnp.where(eye, 1.0, 0.0)
        x = x - jnp.where((row // 2 == col // 2) & (row > col), scaled, 0.0)
        found.append(x)
    k = 2
    while k < window:
        pair = (row // (2 * k) == col // (2 * k)) & (row // k > col // k)
        for w in range(count):
            x = found[w]
            parts = split(x)
            right = dot3(split(jnp.where(pair, diagonals[w][0], 0.0)), parts)
            found[w] = x - dot3(parts, split(right))
        k *= 2
    found = [x * diagonals[w][1] for w, x in enumerate(found)]
    done = {}
    for w in range(count):
        done[w, w] = split(found[w])
        out_ref[0, w * window:(w + 1) * window, w * window:(w + 1) * window] = found[w]
    for gap in range(1, count):
        for c in range(count - gap):
            r = c + gap
            total = None
            for m in range(c, r):
                below = split(l_ref[0, 0, r * window:(r + 1) * window, m * window:(m + 1) * window])
                term = dot3(below, done[m, c])
                total = term if total is None else total + term
            value = -dot3(done[r, r], split(total))
            done[r, c] = split(value)
            out_ref[0, r * window:(r + 1) * window, c * window:(c + 1) * window] = value
            out_ref[0, c * window:(c + 1) * window, r * window:(r + 1) * window] = jnp.zeros(
                (window, window), F32
            )


def inverses(diag_factor):
    levels, size = diag_factor.shape[1], diag_factor.shape[-1]
    return pl.pallas_call(
        functools.partial(inverse_kernel, size, size // 3),
        grid=(levels,),
        in_specs=[pl.BlockSpec((1, 1, size, size), lambda i: (0, i, 0, 0))],
        out_specs=pl.BlockSpec((1, size, size), lambda i: (i, 0, 0)),
        out_shape=jax.ShapeDtypeStruct((levels, size, size), F32),
        compiler_params=pltpu.CompilerParams(vmem_limit_bytes=48 * 2**20),
        name="inverses",
    )(diag_factor)


def nt(a, b):
    return lax.dot_general(a, b, (((1,), (1,)), ((), ())), preferred_element_type=F32)


def nt3(a, b):
    return nt(a[0], b[0]) + (nt(a[1], b[0]) + nt(a[0], b[1]))


def nt2(a, b):
    return nt(a, b[0]) + nt(a, b[1])


def inverse_steps(low, inv, level, starts):
    found, scaled, downs, pairs, eyes = [], [], [], [], []
    for at, to in starts:
        span = to - at
        row = lax.broadcasted_iota(jnp.int32, (span, span), 0)
        col = lax.broadcasted_iota(jnp.int32, (span, span), 1)
        eye = row == col
        block = low[level, at:to, at:to]
        down = 1.0 / jnp.sum(jnp.where(eye, block, 0.0), axis=1, keepdims=True)
        scaled.append(jnp.where(row > col, block * down, 0.0))
        downs.append(down)
        pairs.append(row ^ col)
        eyes.append(jnp.where(eye, 1.0, 0.0))
        first = split(jnp.where(pairs[-1] == 1, scaled[-1], 0.0))
        unit = eyes[-1].astype(BF)
        found.append(eyes[-1] - (nt(unit, first[0]) + nt(unit, first[1])))
    yield
    k = 2
    while k < starts[0][1] - starts[0][0]:
        for w, (at, to) in enumerate(starts):
            if k < to - at:
                parts = split(found[w])
                pair = (pairs[w] >= k) & (pairs[w] < 2 * k)
                right = nt3(parts, split(jnp.where(pair, scaled[w], 0.0)))
                found[w] = found[w] - dot3(split(right), parts)
        k *= 2
        yield
    done = {}

    def keep(c, r, value):
        done[c, r] = split(value)
        rows, columns = slice(*starts[c]), slice(*starts[r])
        inv[0, level, rows, columns] = done[c, r][0]
        inv[1, level, rows, columns] = done[c, r][1]

    for w in range(len(starts)):
        keep(w, w, found[w] * downs[w])
    for gap in range(1, len(starts)):
        for c in range(len(starts) - gap):
            r = c + gap
            total = None
            for m in range(c, r):
                below = split(low[level, slice(*starts[r]), slice(*starts[m])])
                term = nt3(done[c, m], below)
                total = term if total is None else total + term
            keep(c, r, -dot3(split(total), done[r, r]))
            zero = jnp.zeros((starts[r][1] - starts[r][0], starts[c][1] - starts[c][0]), BF)
            inv[0, level, slice(*starts[r]), slice(*starts[c])] = zero
            inv[1, level, slice(*starts[r]), slice(*starts[c])] = zero
        yield


def pack(x):
    rows, columns = x.shape
    full = columns // 128 * 128
    pieces = [x[:, at:at + 128] for at in range(0, full, 128)]
    rest = jnp.concatenate([x[:rows // 2, full:], x[rows // 2:, full:]], axis=1)
    return jnp.concatenate([*pieces, rest], axis=0)


def unpack(x, columns):
    rows = x.shape[0] * 128 // columns
    full = columns // 128
    pieces = [x[i * rows:(i + 1) * rows] for i in range(full)]
    rest = x[full * rows:]
    return jnp.concatenate(
        [*pieces, jnp.concatenate([rest[:, :64], rest[:, 64:]], axis=0)], axis=1
    )


def whole_kernel(size, parts, tiles, root_in, low_in, panel_in, chain_in, panel_out, block_out,
                 low, pf, ch, root, inv, sc, ct, pt, acc, gram, own_sum, sp, g1, g1s, g2, g2s, ar, ars,
                 load_s, pf_s, pf_r, root_s, root_r, fwd_s, fwd_r, sc_s, sc_r, pt_s, pt_r,
                 a_s, a_r, b_s, b_r, x_s, v_s, v_r, out_s, out_r):
    half = size // 2
    step = half // parts
    packed = step * size // 128
    branch = lax.axis_index("branch")
    me = lax.axis_index("row")
    z = me // 2
    core = me % 2
    side = z // 2
    outer, near, across, beyond = 3 * side, 1 + side, 2 - side, 3 - 3 * side
    is_inner = z == near
    is_outer = z == outer
    own = pl.ds(pl.multiple_of(core * half, 32), half)
    sibling = {"row": 2 * z + 1 - core}

    def chip(at):
        return {"row": 2 * at + core}

    def copy(src, dst, send_sem, recv_sem, target):
        return pltpu.make_async_remote_copy(
            src_ref=src, dst_ref=dst, send_sem=send_sem, recv_sem=recv_sem,
            device_id=target, device_id_type=MESH,
        )

    barrier = pltpu.get_barrier_semaphore()
    peers = [sibling] + [chip((z + k) % 4) for k in (1, 2, 3)]
    peers += [{"branch": (branch + k) % 4} for k in (1, 2, 3)]
    for peer in peers:
        pl.semaphore_signal(barrier, inc=1, device_id=peer, device_id_type=MESH)

    loads = {}
    for i in range(3):
        loads["low", i] = pltpu.make_async_copy(low_in.at[0, i], low.at[i], load_s.at[i])
        loads["pf", i] = pltpu.make_async_copy(
            panel_in.at[0, i], pf.at[i, own], load_s.at[3 + i]
        )
    loads["ch", 0] = pltpu.make_async_copy(chain_in.at[0], ch, load_s.at[6])
    loads["root", 0] = pltpu.make_async_copy(root_in, root.at[branch, own], load_s.at[7])
    for key in (("low", 0), ("pf", 0), ("root", 0), ("low", 1), ("low", 2), ("pf", 1), ("pf", 2),
                ("ch", 0)):
        loads[key].start()
    pl.semaphore_wait(barrier, 7)

    pf_to = [
        copy(panel_in.at[0, i], pf.at[i, own], pf_s.at[i], pf_r.at[i], sibling) for i in range(3)
    ]
    root_to = [
        copy(root_in, root.at[branch, own], root_s.at[k - 1], root_r.at[k - 1],
             {"branch": (branch + k) % 4})
        for k in (1, 2, 3)
    ]
    root_own = copy(root_in, root.at[branch, own], fwd_s.at[0], fwd_r.at[0], sibling)
    root_on = []
    for k in (1, 2, 3):
        block = root.at[(branch + 4 - k) % 4, own]
        root_on.append(copy(block, block, fwd_s.at[k], fwd_r.at[k], sibling))
    pf_to[0].start()
    for k in range(3):
        root_to[k].start()
    root_own.start()
    pf_to[1].start()
    pf_to[2].start()

    first, second, third = tiles[0, 0], tiles[0, 1], tiles[0, 2]

    def among(tile, count):
        hit = tile == first
        if count > 1:
            hit = hit | (tile == second)
        if count > 2:
            hit = hit | (tile == third)
        return jnp.where(hit, 1.0, 0.0)

    kept = [among(z, 3), among(z, 2), among(z, 1)]
    near_in, beyond_in = among(near, 3), among(beyond, 3)
    a_index = jnp.where(is_outer & (beyond_in < 0.5), across, beyond)
    b_index = jnp.where(is_outer & (near_in > 0.5), near, across)
    other_index = jnp.where(z == first, second, first)

    bounds = list(range(0, size, 256)) + [size]
    starts = list(zip(bounds[:-1], bounds[1:]))

    def rows(k):
        return slice(k * packed, (k + 1) * packed)

    def own_rows(k):
        return pl.ds(pl.multiple_of(core * half + k * step, 32), step)

    def cut(value, k):
        return value[k * step:(k + 1) * step]

    def whole_of(ref, *index):
        return jnp.concatenate(
            [unpack(ref[(*index, rows(k))].astype(F32), size) for k in range(parts)], axis=0
        )

    def both(ref, *index):
        return ref[(0, *index)], ref[(1, *index)]

    def keep(ref, index, value):
        hi, lo = split(value)
        ref[(0, *index)] = hi
        ref[(1, *index)] = lo

    a_far = [copy(sp.at[0, rows(k)], g1.at[1, rows(k)], a_s.at[0, k], a_r.at[1, k],
                  chip(across)) for k in range(parts)]
    a_near = [copy(sp.at[0, rows(k)], g1.at[0, rows(k)], a_s.at[1, k], a_r.at[0, k],
                   chip(near)) for k in range(parts)]
    b_far = [copy(sp.at[0, rows(k)], g1.at[2, rows(k)], b_s.at[2, k], a_r.at[2, k],
                  chip(across)) for k in range(parts)]
    out_a = [copy(g1s.at[0, rows(k)], g1.at[1, rows(k)], b_s.at[0, k], a_r.at[1, k],
                  chip(outer)) for k in range(parts)]
    out_b = [copy(g1s.at[1, rows(k)], g1.at[2, rows(k)], b_s.at[1, k], a_r.at[2, k],
                  chip(outer)) for k in range(parts)]
    x_near = [copy(sp.at[1, rows(k)], g2.at[0, rows(k)], x_s.at[0, k], b_r.at[0, k],
                   chip(near)) for k in range(parts)]
    x_far = [copy(g2s.at[0, rows(k)], g2.at[1, rows(k)], x_s.at[1, k], b_r.at[1, k],
                  chip(across)) for k in range(parts)]
    x_out = [copy(g2s.at[1, rows(k)], g2.at[1, rows(k)], x_s.at[2, k], b_r.at[1, k],
                  chip(outer)) for k in range(parts)]
    steps = [(m, k) for m in range(5) for k in range(parts)]
    u_near, u_far, u_out = {}, {}, {}
    for m, k in steps:
        u_near[m, k] = copy(ars.at[0, m, rows(k)], ar.at[0, m, rows(k)], v_s.at[0, m, k],
                            v_r.at[0, m, k], chip(near))
        u_far[m, k] = copy(ars.at[0, m, rows(k)], ar.at[1, m, rows(k)], v_s.at[0, m, k],
                           v_r.at[1, m, k], chip(across))
        u_out[m, k] = copy(ars.at[1, m, rows(k)], ar.at[1, m, rows(k)], v_s.at[1, m, k],
                           v_r.at[1, m, k], chip(outer))
    sc_to = [copy(sc.at[0, i, own], sc.at[0, i, own], sc_s.at[i], sc_r.at[i], sibling)
             if i else None for i in (0, 1, 2)]
    pt_to = [copy(pt.at[:, i, own], pt.at[:, i, own], pt_s.at[i], pt_r.at[i], sibling)
             for i in range(3)]

    def forward_root(k):
        root_to[k].wait_recv()
        root_on[k].start()

    def relay_one(k):
        @pl.when(is_inner)
        def _():
            a_far[k].wait_recv()
            b_far[k].wait_recv()
            theirs = g1[2, rows(k)].astype(F32)
            g1s[0, rows(k)] = (
                beyond_in * g1[1, rows(k)].astype(F32) + (1.0 - beyond_in) * theirs
            ).astype(BF)
            g1s[1, rows(k)] = (
                near_in * sp[0, rows(k)].astype(F32) + (1.0 - near_in) * theirs
            ).astype(BF)
            out_a[k].start()
            out_b[k].start()

    def near_two(k):
        @pl.when(is_inner)
        def _():
            x_near[k].wait_recv()
            mine = sp[1, rows(k)].astype(F32)
            g2s[0, rows(k)] = (g2[0, rows(k)].astype(F32) + mine).astype(BF)
            x_far[k].start()

    def far_two(k):
        @pl.when(is_inner)
        def _():
            x_out[k].wait_recv()
            mine = sp[1, rows(k)].astype(F32)
            g2s[1, rows(k)] = (g2[1, rows(k)].astype(F32) + mine).astype(BF)
            x_out[k].start()

    def send_sum(m, value):
        for k in range(parts):
            mine = pack(cut(value, k))
            own_sum[m, rows(k)] = mine
            ars[0, m, rows(k)] = mine.astype(BF)

        @pl.when(is_outer)
        def _():
            for k in range(parts):
                u_near[m, k].start()

    def near_sum(m, k):
        @pl.when(is_inner)
        def _():
            u_near[m, k].wait_recv()
            upto = ar[0, m, rows(k)].astype(F32) + own_sum[m, rows(k)]
            ars[0, m, rows(k)] = upto.astype(BF)
            u_far[m, k].start()

    def far_sum(m, k):
        @pl.when(is_inner)
        def _():
            u_out[m, k].wait_recv()
            rest = ar[1, m, rows(k)].astype(F32) + own_sum[m, rows(k)]
            ars[1, m, rows(k)] = rest.astype(BF)
            u_out[m, k].start()
            own_sum[m, rows(k)] = rest + ar[0, m, rows(k)].astype(F32)

    def settle(m, *some):
        @pl.when(is_outer)
        def _():
            for k in some or range(parts):
                u_out[m, k].wait_recv()
                own_sum[m, rows(k)] = own_sum[m, rows(k)] + ar[1, m, rows(k)].astype(F32)

    order = []
    for i in range(len(steps) + 1):
        if i < len(steps):
            order.append((near_sum, *steps[i]))
        if i:
            order.append((far_sum, *steps[i - 1]))
    order.reverse()

    def relay(count):
        for _ in range(min(count, len(order))):
            todo, m, k = order.pop()
            todo(m, k)

    loads["low", 0].wait()
    for _ in inverse_steps(low, inv, 0, starts):
        pass

    def gram_of(i):
        return jnp.concatenate(
            [nt3(both(inv, i, own, slice(at, size)), both(inv, i, slice(at, to), slice(at, size)))
             for at, to in starts], axis=1,
        )

    def chain_of(i):
        hi, lo = split(ch[i])
        for at, to in starts:
            part = nt3(both(inv, i + 1, slice(at, to), slice(at, size)), (hi[:, at:], lo[:, at:]))
            keep(ct, (i, slice(at, to)), part)

    def scale(i):
        loads["pf", i].wait()
        pf_to[i].wait_recv()
        value = nt3(both(inv, i, own), split(pf[i])) * kept[i]
        keep(sc, (i, own), value)
        if i < 2:
            for k in range(parts):
                sp[i, rows(k)] = pack(cut(value, k)).astype(BF)

    scale(0)

    @pl.when(is_outer)
    def _():
        for k in range(parts):
            a_far[k].start()
            a_near[k].start()

    @pl.when(is_inner)
    def _():
        for k in range(parts):
            b_far[k].start()

    loads["low", 1].wait()
    for _ in inverse_steps(low, inv, 1, starts):
        pass
    scale(1)

    @pl.when(is_outer)
    def _():
        for k in range(parts):
            x_near[k].start()

    sc_to[1].start()
    relay_one(0)
    loads["low", 2].wait()
    for turn, _ in enumerate(inverse_steps(low, inv, 2, starts)):
        if turn == 3:
            for k in range(3):
                forward_root(k)
        if turn == 6:
            relay_one(1)
    scale(2)
    sc_to[2].start()
    relay_one(2)
    loads["ch", 0].wait()
    chain_of(0)
    near_two(0)
    chain_of(1)
    loads["root", 0].wait()
    root_own.wait_recv()
    for k in range(3):
        root_on[k].wait_recv()
    acc[...] = nt(sc[0, 0, own], root[z])

    @pl.when(is_inner)
    def _():
        for k in range(parts):
            a_near[k].wait_recv()
        acc[...] += nt(whole_of(g1, 0).astype(BF), root[outer])

    @pl.when(is_outer)
    def _():
        for k in range(parts):
            out_a[k].wait_recv()
            out_b[k].wait_recv()

    acc[...] += nt(whole_of(g1, 1).astype(BF), root[a_index])
    acc[...] += nt(whole_of(g1, 2).astype(BF), root[b_index])
    first_panel = acc[...] * -kept[0]
    keep(pt, (0, own), first_panel)
    pt_to[0].start()
    sc_to[1].wait_recv()
    send_sum(0, nt(pt[0, 0, own], sc[0, 1]) + nt(pt[1, 0, own], sc[0, 1]))
    near_two(1)
    pt_to[0].wait_recv()
    send_sum(1, nt2(sc[0, 0, own], both(pt, 0)))
    near_two(2)
    far_two(0)
    gram[0] = gram_of(0)
    far_two(1)
    gram[1] = gram_of(1)
    far_two(2)

    @pl.when(is_outer)
    def _():
        for k in range(parts):
            x_out[k].wait_recv()
        acc[...] = whole_of(g2, 1)

    @pl.when(is_inner)
    def _():
        acc[...] = whole_of(g2, 0) + whole_of(g2, 1)

    value = nt(sc[0, 1, own], root[z]) + nt(acc[...].astype(BF), root[other_index])
    value = (value + dot3(both(ct, 0, own), both(pt, 0))) * -kept[1]
    keep(pt, (1, own), value)
    pt_to[1].start()
    relay(1)
    sc_to[2].wait_recv()
    acc[...] = nt(pt[0, 1, own], sc[0, 2]) + nt(pt[1, 1, own], sc[0, 2])
    relay(1)
    pt_to[1].wait_recv()
    send_sum(2, nt2(sc[0, 1, own], both(pt, 1)))
    send_sum(3, acc[...])
    relay(2)

    value = nt(sc[0, 2, own], root[z])
    value = (value + dot3(both(ct, 1, own), both(pt, 1))) * -kept[2]
    keep(pt, (2, own), value)
    pt_to[2].start()
    relay(2)
    pt_to[2].wait_recv()
    send_sum(4, nt2(sc[0, 2, own], both(pt, 2)))
    relay(2)
    gram[2] = gram_of(2)
    relay(2)
    pick = jnp.where(
        lax.broadcasted_iota(jnp.int32, (half, size), 1)
        == lax.broadcasted_iota(jnp.int32, (half, size), 0) + core * half,
        1.0, 0.0,
    ).astype(BF)
    for i in range(3):
        panel_out[0, i] = nt(pick, pt[0, i]) + nt(pick, pt[1, i])
        if i:
            relay(2)

    def give(index, value, sem):
        block_out[0, index, own] = value
        block = block_out.at[0, index, own]
        return copy(block, block, out_s.at[sem], out_r.at[sem], sibling)

    gives = {}
    settle(1)
    gives[0] = give(0, gram[0] - whole_of(own_sum, 1), 0)
    gives[0].start()
    relay(2)
    settle(0)
    gives[3] = give(3, -(whole_of(own_sum, 0) + nt3(split(block_out[0, 0, own]), both(ct, 0))), 3)
    gives[3].start()
    relay(2)
    gives[3].wait_recv()
    gram[1] = gram[1] - dot3(both(ct, 0, own), split(block_out[0, 3]))
    relay(2)
    settle(2)
    value = gram[1] - whole_of(own_sum, 2)
    gives[1] = give(1, value, 1)
    gives[1].start()
    relay(2)
    acc[...] = nt3(split(value), both(ct, 1))
    relay(4)
    settle(3)
    gives[4] = give(4, -(whole_of(own_sum, 3) + acc[...]), 4)
    gives[4].start()
    relay(2)
    gives[4].wait_recv()
    gram[2] = gram[2] - dot3(both(ct, 1, own), split(block_out[0, 4]))
    for k in range(parts):
        relay(1 if k else 0)
        settle(4, k)
        at = own_rows(k)
        block_out[0, 2, at] = gram[2, k * step:(k + 1) * step] - unpack(own_sum[4, rows(k)], size)
        block = block_out.at[0, 2, at]
        gives[5 + k] = copy(block, block, out_s.at[5 + k], out_r.at[5 + k], sibling)
        gives[5 + k].start()
    for i in (0, 1):
        gives[i].wait_recv()
    for k in range(parts):
        gives[5 + k].wait_recv()

    for one in [*pf_to, *root_to, root_own, *root_on, sc_to[1], sc_to[2], *pt_to, *gives.values()]:
        one.wait_send()

    @pl.when(is_outer)
    def _():
        for one in [*a_far, *a_near, *x_near, *u_near.values()]:
            one.wait_send()

    @pl.when(is_inner)
    def _():
        for one in [*b_far, *out_a, *out_b, *x_far, *x_out, *u_far.values(), *u_out.values()]:
            one.wait_send()


def whole(root_cov, diag_factor, panel_factor, chain_factor, panel_tiles):
    size = diag_factor.shape[-1]
    half = size // 2
    parts = 3
    line = half * size // 128
    dma = pltpu.SemaphoreType.DMA
    anywhere = pl.BlockSpec(memory_space=pl.ANY)
    inside = pl.BlockSpec(memory_space=pltpu.VMEM)
    vm = pltpu.VMEM
    return pl.pallas_call(
        functools.partial(whole_kernel, size, parts),
        out_shape=(vm((1, 3, half, size), F32), vm((1, 5, size, size), F32)),
        in_specs=[pl.BlockSpec(memory_space=pltpu.SMEM)] + [anywhere] * 4,
        out_specs=(inside, inside),
        scratch_shapes=[
            vm((3, size, size), F32),
            vm((3, size, size), F32),
            vm((2, size, size), F32),
            vm((4, size, size), BF),
            vm((2, 3, size, size), BF),
            vm((2, 3, size, size), BF),
            vm((2, 2, size, size), BF),
            vm((2, 3, size, size), BF),
            vm((half, size), F32),
            vm((3, half, size), F32),
            vm((5, line, 128), F32),
            vm((2, line, 128), BF),
            vm((3, line, 128), BF),
            vm((2, line, 128), BF),
            vm((2, line, 128), BF),
            vm((2, line, 128), BF),
            vm((2, 5, line, 128), BF),
            vm((2, 5, line, 128), BF),
            dma((8,)), dma((3,)), dma((3,)), dma((3,)), dma((3,)), dma((4,)), dma((4,)),
            dma((3,)), dma((3,)), dma((3,)), dma((3,)),
            dma((2, parts)), dma((3, parts)), dma((3, parts)), dma((2, parts)),
            dma((3, parts)), dma((2, 5, parts)), dma((2, 5, parts)), dma((5 + parts,)),
            dma((5 + parts,)),
        ],
        compiler_params=pltpu.CompilerParams(
            collective_id=0, has_side_effects=True, vmem_limit_bytes=52 * 2**20
        ),
        name="whole",
    )(panel_tiles, root_cov, diag_factor, panel_factor, chain_factor)


def on_device(root_cov, diag_factor, panel_factor, chain_factor, panel_tiles):
    node_width = diag_factor.shape[-1]
    rows_here = panel_factor.shape[2]
    per_tile = node_width // rows_here
    row_count = lax.axis_size("row")
    tile_total = row_count // per_tile
    counts = (3 * tile_total // 4, tile_total // 2, tile_total // 4)
    small = row_count == 8 and tile_total == 4 and root_cov.shape[1] == node_width
    if small:
        return whole(root_cov, diag_factor, panel_factor, chain_factor, panel_tiles)
    root_rows = lax.all_gather(root_cov, "branch", axis=1, tiled=True)
    me = lax.axis_index("row")
    my_tile = me // per_tile
    inverse_all = inverses(diag_factor)
    share = -(-node_width // row_count // 8) * 8
    padded = jnp.pad(inverse_all, ((0, 0), (0, share * row_count - node_width), (0, 0)))
    mine = lax.dynamic_slice_in_dim(padded, me * share, share, axis=1)
    chosen = [jnp.any(panel_tiles[0, : counts[i]] == my_tile) for i in range(3)]
    scaled = [
        jnp.where(chosen[i], product(panel_factor[0, i], inverse_all[i]), 0.0) for i in range(3)
    ]
    panels = []
    blocks = []
    crosses = []
    for i in range(3):
        rounded = scaled[i].astype(BF)
        gathered = jnp.dot(
            root_rows,
            lax.all_gather(rounded, "row", axis=0, tiled=True),
            preferred_element_type=F32,
        )
        left = jnp.concatenate([mine[i], scaled[i]], axis=0)
        if i == 0:
            panel = -jnp.where(chosen[i], gathered, 0.0)
            block = product(left.T, jnp.concatenate([mine[i], -panel], axis=0))
        else:
            chain = product(chain_factor[0, i - 1], inverse_all[i])
            panel = -jnp.where(chosen[i], gathered + product(panels[-1], chain), 0.0)
            cross = -(product(panels[-1].T, scaled[i]) + product(blocks[-1], chain))
            block = product(left.T, jnp.concatenate([mine[i], -panel], axis=0)) - product(
                chain.T, cross
            )
            crosses.append(cross)
        panels.append(panel)
        blocks.append(block)
    total = lax.psum(jnp.stack(blocks + crosses), "row")
    return (jnp.stack(panels)[None], total[None])


def solution(mesh):
    in_specs = (
        P("row", "branch"),
        P("branch", None, None, None),
        P("branch", None, "row", None),
        P("branch", None, None, None),
        P("branch", None),
    )
    out_specs = (P("branch", None, "row", None), P("branch", None, None, None))
    return jax.shard_map(
        on_device, mesh=mesh, in_specs=in_specs, out_specs=out_specs, check_vma=False
    )
```
